32 devices in a mesh: band: 8 (over y, x, core), grid: 4 (over z).
Axes of the slice: x: 2, y: 2, z: 4, core: 2. Of those that a mesh axis runs over, the one named last changes fastest.
Arguments:
- orbitals: bfloat16 [64, 72, 5184], P('band', 'grid'), may hold values from -6 to 6
- owners: int32 [2], replicated, may hold values from 0 to 7, as said below
Outputs:
- exchange_field: float32 [64, 72, 5184], P('band', 'grid')
The draws below stay inside these ranges and needn't reach their ends.
Inputs may be any that keep to these rules, and one draw needn't show every extreme that they name: owners[r] names a band group; the rounds name distinct groups.
All inputs are finite; a program needn't handle non-finite values.
Results may differ from the reference program's by a relative error of at most 0.0077.
Values may be sent and summed in bfloat16 or wider, within the bound.
No kernel may reach another device: no remote copies, remote signals or barrier semaphores. Data moves between devices by JAX's collectives and lax.ppermute only.
A program may use at most 128 MiB of HBM per device.

```python
import math
import jax
import jax.numpy as jnp
from jax import lax

NG = 72
BAND_DEV = 8
ROUNDS = 2
BANDS = 64
N_BAND = 8


def draw_owners(key, part):
    key = jax.random.fold_in(key, 11)
    order_key, shift_key = jax.random.split(key)
    others = jax.random.permutation(order_key, N_BAND - 1)
    chosen = jnp.concatenate([jnp.array([N_BAND - 1], dtype=jnp.int32), others[:ROUNDS - 1].astype(jnp.int32)])
    offset = jax.random.randint(shift_key, (), 0, ROUNDS)
    return jnp.roll(chosen, offset).astype(jnp.int32)


def block_levels(own_key, dims, pieces, low, largest):
    def one(dim, shards_of):
        draws = jax.random.uniform(jax.random.fold_in(jax.random.fold_in(own_key, 6), dim), (shards_of,), jnp.float32, low / len(pieces), largest / len(pieces))
        return jnp.repeat(jnp.exp(draws), dims[dim] // shards_of).reshape((-1,) + (1,) * (len(dims) - dim - 1))

    level = one(*pieces[0])
    for cut in pieces[1:]:
        level = level * one(*cut)
    return level


def scatter_about(stream_key, shape, width, most, cuts=(), held_as=jnp.bfloat16):
    result = jax.random.normal(stream_key, shape, jnp.float32) * width
    if len(cuts) > 0:
        result = block_levels(stream_key, shape, cuts, -0.22, 0.18) * result
    return jnp.clip(result, min=-most, max=most).astype(held_as)


def setup_inputs(seed: int = 0) -> dict:
    key_list = jax.random.split(jax.random.key(seed), 3)
    orbitals = scatter_about(key_list[0], (BANDS, NG, NG * NG), 1.0, 6.0, ((0, 8), (1, 4)))
    owners = draw_owners(jax.random.fold_in(key_list[2], 71), 0)
    return {"orbitals": orbitals, "owners": owners}


box_length = 12.0
screening = 0.106


def cas_table(length):
    points = jnp.arange(length, dtype=jnp.int32)
    products = (points[:, None] * points[None, :]) % length
    phase = products.astype(jnp.float32) * (2.0 * math.pi / length)
    return (jnp.cos(phase) + jnp.sin(phase)).astype(jnp.bfloat16)


def screened_kernel(length):
    points = jnp.arange(length, dtype=jnp.int32)
    folded = jnp.minimum(points, length - points).astype(jnp.float32)
    squares = folded * folded
    factor = (2.0 * math.pi / box_length) ** 2
    wave_sq = factor * (squares[:, None, None] + squares[None, :, None] + squares[None, None, :])
    positive = jnp.where(wave_sq > 0.0, wave_sq, 1.0)
    screen = 4.0 * math.pi * (1.0 - jnp.exp(-positive / (4.0 * screening * screening))) / positive
    screen = screen / float(length * length * length)
    return jnp.where(wave_sq > 0.0, screen, 0.0).astype(jnp.float32)


def solve_pairs(density, table, kernel):
    f32 = jnp.float32
    first = jnp.einsum('pxyz,cz->pxyc', density.astype(f32), table).astype(jnp.bfloat16)
    second = jnp.einsum('pxyc,by->pxbc', first.astype(f32), table).astype(jnp.bfloat16)
    third = (jnp.einsum('pxbc,ax->pabc', second.astype(f32), table) * kernel[None]).astype(jnp.bfloat16)
    fourth = jnp.einsum('pabc,xa->pxbc', third.astype(f32), table).astype(jnp.bfloat16)
    fifth = jnp.einsum('pxbc,yb->pxyc', fourth.astype(f32), table).astype(jnp.bfloat16)
    return jnp.einsum('pxyc,zc->pxyz', fifth.astype(f32), table)


def reference(orbitals, owners):
    table = cas_table(NG).astype(jnp.float32)
    kernel = screened_kernel(NG)
    full = orbitals.reshape(BANDS, NG, NG, NG)
    blocks = full.reshape(N_BAND, BAND_DEV, NG, NG, NG)
    accumulated = jnp.zeros((N_BAND, BAND_DEV, NG, NG, NG), jnp.float32)
    for round_number in range(ROUNDS):
        start = (owners[round_number] * BAND_DEV).astype(jnp.int32)
        owner_set = lax.dynamic_slice_in_dim(full, start, BAND_DEV, 0)

        def per_block(band_block):
            def update(running, orbital):
                density = (band_block.astype(jnp.float32) * orbital.astype(jnp.float32)[None]).astype(jnp.bfloat16)
                potential = solve_pairs(density, table, kernel)
                return running + potential * orbital.astype(jnp.float32)[None], None

            start_value = jnp.zeros((BAND_DEV, NG, NG, NG), jnp.float32)
            running, _ = lax.scan(update, start_value, owner_set)
            return running

        accumulated = accumulated + lax.map(per_block, blocks)
    return accumulated.reshape(BANDS, NG, NG * NG)
```

```python
import functools
import math

import jax
import jax.numpy as jnp
import numpy as np
from jax import lax
from jax.experimental import pallas as pl
from jax.experimental.pallas import tpu as pltpu
from jax.sharding import PartitionSpec as P

box_length = 12.0
screening = 0.106
BF16 = jnp.bfloat16
F32 = jnp.float32
LANES = 256
HALF = 128
PACK = 3


def cas_table(length):
    points = np.arange(length)
    products = points[:, None] * points[None, :] % length
    phase = products.astype(np.float32) * np.float32(2.0 * math.pi / length)
    return (np.cos(phase) + np.sin(phase)).astype(BF16)


def screened_kernel(length):
    points = np.arange(length)
    folded = np.minimum(points, length - points).astype(np.float32)
    squares = folded * folded
    factor = np.float32((2.0 * math.pi / box_length) ** 2)
    wave_sq = factor * (squares[:, None, None] + squares[None, :, None] + squares[None, None, :])
    positive = np.where(wave_sq > 0.0, wave_sq, np.float32(1.0))
    screen = np.float32(4.0 * math.pi) * (
        np.float32(1.0) - np.exp(-positive / np.float32(4.0 * screening * screening))
    )
    screen = screen / positive / np.float32(length**3)
    return np.where(wave_sq > 0.0, screen, np.float32(0.0)).astype(np.float32)


def padded(array, width):
    return np.pad(array, [(0, 0)] * (array.ndim - 1) + [(0, width - array.shape[-1])])


def pack(bands):
    count, planes, side, _ = bands.shape
    split = bands.reshape(count, planes // 6, 2, PACK, side, side).transpose(0, 1, 2, 4, 3, 5)
    joined = split.reshape(count, planes // 6, 2 * side, PACK * side)
    return jnp.pad(joined, ((0, 0), (0, 0), (0, 0), (0, LANES - PACK * side)))


def unpack(packed, side):
    count, steps = packed.shape[:2]
    split = packed[..., : PACK * side].reshape(count, steps, 2, side, PACK, side)
    return split.transpose(0, 1, 2, 4, 3, 5).reshape(count, steps * 6, side, side)


def dot(left, right):
    return lax.dot_general(left, right, (((1,), (0,)), ((), ())), preferred_element_type=F32)


def swap_thirds(values, side):
    pad = jnp.zeros((values[0].shape[0], LANES - PACK * side), values[0].dtype)
    return [
        jnp.concatenate([v[:, side * s : side * s + side] for v in values] + [pad], axis=1)
        for s in range(PACK)
    ]


def make_groups(own_count, band_count):
    groups, left = [], []
    for own in range(own_count):
        full = band_count // PACK * PACK
        for j in range(0, full, PACK):
            groups.append(tuple((own, j + k) for k in range(PACK)))
        left += [(own, j) for j in range(full, band_count)]
    for start in range(0, len(left), PACK):
        groups.append(tuple(left[start : start + PACK]))
    return groups


def solve_body(*refs, side, pitch, sizes, groups, has_start):
    own_ref = refs[0]
    band_refs = refs[1 : 1 + len(sizes)]
    rest = refs[1 + len(sizes) :]
    if has_start:
        start_ref, rest = rest[0], rest[1:]
    kernel_ref, cas2_ref, ahead_ref, back_ref, thirds_ref, total_ref, low, high = rest
    where = [(ref, k) for ref, size in zip(band_refs, sizes) for k in range(size)]
    steps = own_ref.shape[1]
    half = side // 2
    wide = math.gcd(steps, 4)
    many = next(k for k in (12, 9, 6, 4, 3, 2, 1) if half % k == 0)

    def band(j, step):
        return where[j][0][where[j][1], step]

    def put(plane, value):
        low[pl.ds(plane * pitch, side), :] = value[:, :HALF]
        high[pl.ds(plane * pitch, side), :] = value[:, HALF:]

    def get(plane):
        parts = [r[pl.ds(plane * pitch, side), :] for r in (low, high)]
        return jnp.concatenate(parts, axis=1)

    def put_across(row, value):
        low[pl.ds(row, side, stride=pitch), :] = value[:, :HALF]
        high[pl.ds(row, side, stride=pitch), :] = value[:, HALF:]

    def get_across(row):
        parts = [r[pl.ds(row, side, stride=pitch), :] for r in (low, high)]
        return jnp.concatenate(parts, axis=1)

    if has_start:
        total_ref[...] = start_ref[...]
    else:
        total_ref[...] = jnp.zeros_like(total_ref)
    for pairs in groups:
        full = tuple(pairs) + (pairs[-1],) * (PACK - len(pairs))

        def first_two(q, carry):
            work = []
            for w in range(wide):
                step = q * wide + w
                density = [own_ref[i, step] * band(j, step) for i, j in full]
                work += [(6 * step + s, v) for s, v in enumerate(swap_thirds(density, side))]
            along_z = [dot(v, thirds_ref[...]).astype(BF16) for _, v in work]
            along_y = [dot(cas2_ref[...], v) for v in along_z]
            for (plane, _), v in zip(work, along_y):
                put(plane, v[:side])
                put(plane + PACK, v[side:])
            return carry

        def middle_two(q, carry):
            rows = [q * many + w for w in range(many)]
            planes = [
                jnp.concatenate([get_across(2 * r), get_across(2 * r + 1)], axis=0).astype(BF16)
                for r in rows
            ]
            waves = [dot(ahead_ref[...], v) for v in planes]
            waves = [(v * kernel_ref[r]).astype(BF16) for r, v in zip(rows, waves)]
            planes = [dot(back_ref[...], v) for v in waves]
            for r, v in zip(rows, planes):
                put_across(2 * r, v[:side])
                put_across(2 * r + 1, v[side:])
            return carry

        def last_two(q, carry):
            work = [q * wide + w for w in range(wide)]
            halves = [
                [
                    jnp.concatenate([get(6 * t + s), get(6 * t + PACK + s)], axis=0).astype(BF16)
                    for s in range(PACK)
                ]
                for t in work
            ]
            along_y = [[dot(cas2_ref[...], v).astype(BF16) for v in vs] for vs in halves]
            swapped = [swap_thirds(vs, side) for vs in along_y]
            potential = [[dot(v, thirds_ref[...]) for v in vs[: len(pairs)]] for vs in swapped]
            for t, vs in zip(work, potential):
                sums = {}
                for (i, j), v in zip(pairs, vs):
                    term = v * band(j, t).astype(F32)
                    sums[i] = sums[i] + term if i in sums else term
                for i, v in sums.items():
                    total_ref[i, t] += v
            return carry

        lax.fori_loop(0, steps // wide, first_two, 0)
        lax.fori_loop(0, half // many, middle_two, 0)
        lax.fori_loop(0, steps // wide, last_two, 0)


def solve(own, bands, start, tables, side):
    sizes = [b.shape[0] for b in bands]
    count = own.shape[0]
    groups = make_groups(count, sum(sizes))
    pitch = side + 4
    vmem = pl.BlockSpec(memory_space=pltpu.VMEM)
    operands = [own, *bands] + ([] if start is None else [start]) + list(tables)
    body = functools.partial(
        solve_body, side=side, pitch=pitch, sizes=sizes, groups=groups, has_start=start is not None
    )
    pairs = count * sum(sizes)
    return pl.pallas_call(
        body,
        in_specs=[vmem] * len(operands),
        out_specs=vmem,
        out_shape=jax.ShapeDtypeStruct(own.shape, F32),
        scratch_shapes=[pltpu.VMEM((side * pitch, HALF), F32)] * 2,
        compiler_params=pltpu.CompilerParams(vmem_limit_bytes=60 * 2**20),
        cost_estimate=pl.CostEstimate(
            flops=pairs * 12 * side**4 * 4, bytes_accessed=10 * 2**20, transcendentals=0
        ),
    )(*operands)


def make_tables(side, slab, level):
    cas = cas_table(side)
    two = np.eye(2, dtype=np.float32)
    cas2 = jnp.asarray(np.kron(two, cas.astype(np.float32)).astype(BF16))
    three = np.kron(np.eye(PACK, dtype=np.float32), cas.astype(np.float32))
    margin = LANES - three.shape[0]
    thirds = jnp.asarray(np.pad(three, ((0, margin), (0, margin))).astype(BF16))
    screen = screened_kernel(side).transpose(1, 0, 2)
    screen = padded(np.concatenate([screen] * PACK, axis=-1), LANES)
    screen = jnp.asarray(screen.reshape(side // 2, 2 * side, LANES))
    table = jnp.asarray(cas)
    moved = lax.dynamic_slice_in_dim(jnp.concatenate([table, table], 0), level * slab, side, 0)
    zero = jnp.zeros_like(moved)
    back = jnp.concatenate(
        [jnp.concatenate([moved, zero], 1), jnp.concatenate([zero, moved], 1)], 0
    )
    return screen, cas2, back.T, back, thirds


def from_level(value, ahead):
    count = lax.axis_size("grid")
    pairs = [((h + ahead) % count, h) for h in range(count)]
    return lax.ppermute(value, "grid", pairs)


def flip(value, bit):
    return lax.ppermute(value, "band", [(b, b ^ bit) for b in range(lax.axis_size("band"))])


def pick(options, index):
    result = options[0]
    for k in range(1, len(options)):
        result = jnp.where(index == k, options[k], result)
    return result


def own_bands(packed, per_device):
    levels = lax.axis_size("grid")
    level = lax.axis_index("grid")
    pieces = []
    for ahead in range(levels):
        start = (level + levels - ahead) % levels * per_device
        piece = lax.dynamic_slice_in_dim(packed, start, per_device, 0)
        pieces.append(from_level(piece, ahead) if ahead else piece)
    return jnp.concatenate(pieces, axis=1)


def whole(slab):
    levels = lax.axis_size("grid")
    pieces = [slab] + [from_level(slab, ahead) for ahead in range(1, levels)]
    return jnp.concatenate(pieces, axis=1)


def fields_small(packed, owners, own, tables, side):
    band = lax.axis_index("band")
    core, line = band % 2, band // 2
    share = packed.shape[0] // 4
    parts = []
    for k in range(4):
        part = lax.dynamic_slice_in_dim(packed, (line ^ k) * share, share, 0)
        parts.append(flip(part, 2 * k) if k else part)
    here = owners[core]
    there = owners[1 - core]
    mine = pick(parts, line ^ (here // 2))
    other = flip(pick(parts, line ^ (there // 2)), 1)
    mine = whole(jnp.where(here % 2 == core, mine, other))
    mine_x, mine_y = flip(mine, 2), flip(mine, 4)
    cut = share // 2
    corner = [flip(mine_x[:cut], 4), flip(mine_y[cut:], 2)]
    total = solve(own, [mine, flip(mine, 1)], None, tables, side)
    total = solve(own, [mine_x, mine_y, flip(mine_x, 1), flip(mine_y, 1)], total, tables, side)
    return solve(own, corner + [flip(c, 1) for c in corner], total, tables, side)


def fields_any(packed, owners, own, tables, side):
    total = None
    band = lax.axis_index("band")
    for r in range(owners.shape[0]):
        kept = jnp.where(band == owners[r], packed, jnp.zeros_like(packed))
        bands = whole(lax.psum(kept, "band"))
        total = solve(own, [bands], total, tables, side)
    return total


def body(orbitals, owners):
    band_count, slab, plane = orbitals.shape
    levels = lax.axis_size("grid")
    level = lax.axis_index("grid")
    side = slab * levels
    per_device = band_count // levels
    tables = make_tables(side, slab, level)
    packed = pack(orbitals.reshape(band_count, slab, side, side))
    own = own_bands(packed, per_device)
    small = lax.axis_size("band") == 8 and owners.shape[0] == 2 and band_count % 8 == 0
    fields = (fields_small if small else fields_any)(packed, owners, own, tables, side)
    fields = fields.astype(BF16)
    steps = slab // 6
    pieces = []
    for ahead in range(levels):
        behind = (levels - ahead) % levels
        piece = fields[:, behind * steps : (behind + 1) * steps]
        pieces.append(from_level(piece, ahead) if ahead else piece)
    ordered = jnp.concatenate(pieces + pieces, axis=0)
    ordered = lax.dynamic_slice_in_dim(ordered, (levels - level) * per_device, band_count, 0)
    return unpack(ordered, side).astype(F32).reshape(band_count, slab, plane)


def solution(mesh):
    placed = (P("band", "grid", None), P())
    return jax.shard_map(
        body, mesh=mesh, in_specs=placed, out_specs=P("band", "grid", None), check_vma=False
    )
```

```python
import functools
import math

import jax
import jax.numpy as jnp
import numpy as np
from jax import lax
from jax.experimental import pallas as pl
from jax.experimental.pallas import tpu as pltpu
from jax.sharding import PartitionSpec as P

box_length = 12.0
screening = 0.106
BF16 = jnp.bfloat16
F32 = jnp.float32
LANES = 256
HALF = 128
PACK = 3


def cas_table(length):
    points = np.arange(length)
    products = points[:, None] * points[None, :] % length
    phase = products.astype(np.float32) * np.float32(2.0 * math.pi / length)
    return (np.cos(phase) + np.sin(phase)).astype(BF16)


def screened_kernel(length):
    points = np.arange(length)
    folded = np.minimum(points, length - points).astype(np.float32)
    squares = folded * folded
    factor = np.float32((2.0 * math.pi / box_length) ** 2)
    wave_sq = factor * (squares[:, None, None] + squares[None, :, None] + squares[None, None, :])
    positive = np.where(wave_sq > 0.0, wave_sq, np.float32(1.0))
    screen = np.float32(4.0 * math.pi) * (
        np.float32(1.0) - np.exp(-positive / np.float32(4.0 * screening * screening))
    )
    screen = screen / positive / np.float32(length**3)
    return np.where(wave_sq > 0.0, screen, np.float32(0.0)).astype(np.float32)


def padded(array, width):
    return np.pad(array, [(0, 0)] * (array.ndim - 1) + [(0, width - array.shape[-1])])


def pack_body(in_ref, out_ref, rows, *, side):
    slab, plane = in_ref.shape[1:]
    pitch = rows.shape[0] // slab
    values = in_ref[0].astype(F32)
    for y in range(side):
        rows[pl.ds(y, slab, stride=pitch), pl.ds(0, side)] = values[:, y * side : (y + 1) * side]
    pad = jnp.zeros((2 * side, LANES - PACK * side), BF16)
    for step in range(slab // 6):
        parts = []
        for s in range(PACK):
            both = [rows[pl.ds((6 * step + PACK * e + s) * pitch, side), :][:, :side] for e in range(2)]
            parts.append(jnp.concatenate(both, axis=0).astype(BF16))
        out_ref[0, step] = jnp.concatenate(parts + [pad], axis=1)

def pack(orbitals, side):
    count, slab, plane = orbitals.shape
    return pl.pallas_call(
        functools.partial(pack_body, side=side),
        grid=(count,),
        in_specs=[pl.BlockSpec((1, slab, plane), lambda b: (b, 0, 0))],
        out_specs=pl.BlockSpec((1, slab // 6, 2 * side, LANES), lambda b: (b, 0, 0, 0)),
        out_shape=jax.ShapeDtypeStruct((count, slab // 6, 2 * side, LANES), BF16),
        scratch_shapes=[pltpu.VMEM((slab * (side+4), HALF), F32)],
        compiler_params=pltpu.CompilerParams(vmem_limit_bytes=32 * 2**20),
    )(orbitals)

def unpack_body(level_ref, *refs, side):
    pieces, (out_ref, rows) = refs[:-2], refs[-2:]
    slab = out_ref.shape[1]
    pitch = rows.shape[0] // slab
    ahead, band = pl.program_id(0), pl.program_id(1)
    for k, piece in enumerate(pieces):
        @pl.when(ahead == k)
        def _():
            for step in range(slab // 6):
                value = piece[band, step].astype(F32)
                for s in range(PACK):
                    part = value[:, s * side : (s + 1) * side]
                    for e in range(2):
                        start = (6 * step + PACK * e + s) * pitch
                        rows[pl.ds(start, side), pl.ds(0, side)] = part[e * side : (e + 1) * side]
    parts = [rows[pl.ds(y, slab, stride=pitch), :][:, :side] for y in range(side)]
    out_ref[0] = jnp.concatenate(parts, axis=1)

def unpack(pieces, level, side):
    levels = len(pieces)
    share, steps = pieces[0].shape[:2]
    slab = steps * 6
    grid_spec = pltpu.PrefetchScalarGridSpec(
        num_scalar_prefetch=1,
        grid=(levels, share),
        in_specs=[pl.BlockSpec(memory_space=pltpu.VMEM)] * levels,
        out_specs=pl.BlockSpec((1, slab, side * side), lambda k, b, lv: ((lv[0] + k) % levels * share + b, 0, 0)),
        scratch_shapes=[pltpu.VMEM((slab * (side+4), HALF), F32)],
    )
    return pl.pallas_call(
        functools.partial(unpack_body, side=side),
        grid_spec=grid_spec,
        out_shape=jax.ShapeDtypeStruct((levels * share, slab, side * side), F32),
        compiler_params=pltpu.CompilerParams(vmem_limit_bytes=32 * 2**20),
    )(jnp.reshape(level, (1,)), *pieces)
def dot(left, right):
    return lax.dot_general(left, right, (((1,), (0,)), ((), ())), preferred_element_type=F32)


def swap_thirds(values, side):
    pad = jnp.zeros((values[0].shape[0], LANES - PACK * side), values[0].dtype)
    return [
        jnp.concatenate([v[:, side * s : side * s + side] for v in values] + [pad], axis=1)
        for s in range(PACK)
    ]


def make_groups(own_count, band_count):
    groups, left = [], []
    for own in range(own_count):
        full = band_count // PACK * PACK
        for j in range(0, full, PACK):
            groups.append(tuple((own, j + k) for k in range(PACK)))
        left += [(own, j) for j in range(full, band_count)]
    for start in range(0, len(left), PACK):
        groups.append(tuple(left[start : start + PACK]))
    return groups


def solve_body(*refs, side, pitch, sizes, groups, has_start, cuts):
    own_ref = refs[0]
    band_refs = refs[1 : 1 + len(sizes)]
    rest = refs[1 + len(sizes) :]
    if has_start:
        start_ref, rest = rest[0], rest[1:]
    kernel_ref, cas2_ref, ahead_ref, back_ref, thirds_ref = rest[:5]
    out_refs, (low, high, *totals) = rest[5 : 5 + cuts], rest[5 + cuts :]
    total_ref = totals[0] if totals else out_refs[0]
    where = [(ref, k) for ref, size in zip(band_refs, sizes) for k in range(size)]
    steps = own_ref.shape[1]
    half = side // 2
    wide = math.gcd(steps, 4)
    many = next(k for k in (12, 9, 6, 4, 3, 2, 1) if half % k == 0)

    def band(j, step):
        return where[j][0][where[j][1], step]

    def put(plane, value):
        low[pl.ds(plane * pitch, side), :] = value[:, :HALF]
        high[pl.ds(plane * pitch, side), :] = value[:, HALF:]

    def get(plane):
        parts = [r[pl.ds(plane * pitch, side), :] for r in (low, high)]
        return jnp.concatenate(parts, axis=1)

    def put_across(row, value):
        low[pl.ds(row, side, stride=pitch), :] = value[:, :HALF]
        high[pl.ds(row, side, stride=pitch), :] = value[:, HALF:]

    def get_across(row):
        parts = [r[pl.ds(row, side, stride=pitch), :] for r in (low, high)]
        return jnp.concatenate(parts, axis=1)

    if has_start:
        total_ref[...] = start_ref[...]
    else:
        total_ref[...] = jnp.zeros_like(total_ref)
    for pairs in groups:
        full = tuple(pairs) + (pairs[-1],) * (PACK - len(pairs))

        def first_two(q, carry):
            work = []
            for w in range(wide):
                step = q * wide + w
                density = [own_ref[i, step] * band(j, step) for i, j in full]
                work += [(6 * step + s, v) for s, v in enumerate(swap_thirds(density, side))]
            along_z = [dot(v, thirds_ref[...]).astype(BF16) for _, v in work]
            along_y = [dot(cas2_ref[...], v) for v in along_z]
            for (plane, _), v in zip(work, along_y):
                put(plane, v[:side])
                put(plane + PACK, v[side:])
            return carry

        def middle_two(q, carry):
            rows = [q * many + w for w in range(many)]
            planes = [
                jnp.concatenate([get_across(2 * r), get_across(2 * r + 1)], axis=0).astype(BF16)
                for r in rows
            ]
            waves = [dot(ahead_ref[...], v) for v in planes]
            waves = [(v * kernel_ref[r]).astype(BF16) for r, v in zip(rows, waves)]
            planes = [dot(back_ref[...], v) for v in waves]
            for r, v in zip(rows, planes):
                put_across(2 * r, v[:side])
                put_across(2 * r + 1, v[side:])
            return carry

        def last_two(q, carry):
            work = [q * wide + w for w in range(wide)]
            halves = [
                [
                    jnp.concatenate([get(6 * t + s), get(6 * t + PACK + s)], axis=0).astype(BF16)
                    for s in range(PACK)
                ]
                for t in work
            ]
            along_y = [[dot(cas2_ref[...], v).astype(BF16) for v in vs] for vs in halves]
            swapped = [swap_thirds(vs, side) for vs in along_y]
            potential = [[dot(v, thirds_ref[...]) for v in vs[: len(pairs)]] for vs in swapped]
            for t, vs in zip(work, potential):
                sums = {}
                for (i, j), v in zip(pairs, vs):
                    term = v * band(j, t).astype(F32)
                    sums[i] = sums[i] + term if i in sums else term
                for i, v in sums.items():
                    total_ref[i, t] += v
            return carry

        lax.fori_loop(0, steps // wide, first_two, 0)
        lax.fori_loop(0, half // many, middle_two, 0)
        lax.fori_loop(0, steps // wide, last_two, 0)
    if totals:
        for k, out_ref in enumerate(out_refs):
            size = out_ref.shape[1]
            out_ref[...] = total_ref[:, k * size : (k + 1) * size].astype(out_ref.dtype)


def solve(own, bands, start, tables, side, cuts=0):
    sizes = [b.shape[0] for b in bands]
    count = own.shape[0]
    groups = make_groups(count, sum(sizes))
    pitch = side + 4
    vmem = pl.BlockSpec(memory_space=pltpu.VMEM)
    operands = [own, *bands] + ([] if start is None else [start]) + list(tables)
    body = functools.partial(
        solve_body, side=side, pitch=pitch, sizes=sizes, groups=groups,
        has_start=start is not None, cuts=max(cuts, 1)
    )
    totals = [pltpu.VMEM(own.shape, F32)] if cuts else []
    piece = (count, own.shape[1] // max(cuts, 1)) + own.shape[2:]
    piece = jax.ShapeDtypeStruct(piece, BF16)
    pairs = count * sum(sizes)
    return pl.pallas_call(
        body,
        in_specs=[vmem] * len(operands),
        out_specs=[vmem] * cuts if cuts else vmem,
        out_shape=[piece] * cuts if cuts else jax.ShapeDtypeStruct(own.shape, F32),
        scratch_shapes=[pltpu.VMEM((side * pitch, HALF), F32)] * 2 + totals,
        compiler_params=pltpu.CompilerParams(vmem_limit_bytes=60 * 2**20),
        cost_estimate=pl.CostEstimate(
            flops=pairs * 12 * side**4 * 4, bytes_accessed=10 * 2**20, transcendentals=0
        ),
    )(*operands)


def make_tables(side, slab, level):
    cas = cas_table(side)
    two = np.eye(2, dtype=np.float32)
    cas2 = jnp.asarray(np.kron(two, cas.astype(np.float32)).astype(BF16))
    three = np.kron(np.eye(PACK, dtype=np.float32), cas.astype(np.float32))
    margin = LANES - three.shape[0]
    thirds = jnp.asarray(np.pad(three, ((0, margin), (0, margin))).astype(BF16))
    screen = screened_kernel(side).transpose(1, 0, 2)
    screen = padded(np.concatenate([screen] * PACK, axis=-1), LANES)
    screen = jnp.asarray(screen.reshape(side // 2, 2 * side, LANES))
    table = jnp.asarray(cas)
    moved = lax.dynamic_slice_in_dim(jnp.concatenate([table, table], 0), level * slab, side, 0)
    zero = jnp.zeros_like(moved)
    back = jnp.concatenate(
        [jnp.concatenate([moved, zero], 1), jnp.concatenate([zero, moved], 1)], 0
    )
    return screen, cas2, back.T, back, thirds


def from_level(value, ahead):
    count = lax.axis_size("grid")
    pairs = [((h + ahead) % count, h) for h in range(count)]
    return lax.ppermute(value, "grid", pairs)


def flip(value, bit):
    return lax.ppermute(value, "band", [(b, b ^ bit) for b in range(lax.axis_size("band"))])


def pick(options, index):
    result = options[0]
    for k in range(1, len(options)):
        result = jnp.where(index == k, options[k], result)
    return result


def own_bands(packed, per_device):
    levels = lax.axis_size("grid")
    level = lax.axis_index("grid")
    pieces = []
    for ahead in range(levels):
        start = (level + levels - ahead) % levels * per_device
        piece = lax.dynamic_slice_in_dim(packed, start, per_device, 0)
        pieces.append(from_level(piece, ahead) if ahead else piece)
    return pieces


def whole(slab):
    levels = lax.axis_size("grid")
    pieces = [slab] + [from_level(slab, ahead) for ahead in range(1, levels)]
    return jnp.concatenate(pieces, axis=1)


def fields_small(packed, owners, own, tables, side):
    band = lax.axis_index("band")
    core, line = band % 2, band // 2
    share = packed.shape[0] // 4
    parts = []
    for k in range(4):
        part = lax.dynamic_slice_in_dim(packed, (line ^ k) * share, share, 0)
        parts.append(flip(part, 2 * k) if k else part)
    parts, own = lax.optimization_barrier((parts, own))
    own = jnp.concatenate(own, axis=1)
    here = owners[core]
    there = owners[1 - core]
    mine = pick(parts, line ^ (here // 2))
    other = flip(pick(parts, line ^ (there // 2)), 1)
    mine = jnp.where(here % 2 == core, mine, other)
    mine = whole(mine)
    mine_x, mine_y = flip(mine, 2), flip(mine, 4)
    total = solve(own, [mine, flip(mine, 1)], None, tables, side)
    total, mine_x, mine_y = lax.optimization_barrier((total, mine_x, mine_y))
    cut = share // 2
    corner = [flip(mine_x[:cut], 4), flip(mine_y[cut:], 2)]
    total = solve(own, [mine_x, mine_y, flip(mine_x, 1), flip(mine_y, 1)], total, tables, side)
    total, *corner = lax.optimization_barrier((total, *corner))
    levels = lax.axis_size("grid")
    return solve(own, corner + [flip(c, 1) for c in corner], total, tables, side, levels)


def fields_any(packed, owners, own, tables, side):
    total = None
    band = lax.axis_index("band")
    levels = lax.axis_size("grid")
    own = jnp.concatenate(own, axis=1)
    for r in range(owners.shape[0]):
        cuts = levels if r == owners.shape[0] - 1 else 0
        kept = jnp.where(band == owners[r], packed, jnp.zeros_like(packed))
        bands = whole(lax.psum(kept, "band"))
        total = solve(own, [bands], total, tables, side, cuts)
    return total


def body(orbitals, owners):
    band_count, slab, plane = orbitals.shape
    levels = lax.axis_size("grid")
    level = lax.axis_index("grid")
    side = slab * levels
    per_device = band_count // levels
    tables = make_tables(side, slab, level)
    packed = pack(orbitals, side)
    own = own_bands(packed, per_device)
    small = lax.axis_size("band") == 8 and owners.shape[0] == 2 and band_count % 8 == 0
    fields = (fields_small if small else fields_any)(packed, owners, own, tables, side)
    pieces = []
    for ahead in range(levels):
        piece = fields[(levels - ahead) % levels]
        pieces.append(from_level(piece, ahead) if ahead else piece)
    return unpack(pieces, level, side)


def solution(mesh):
    placed = (P("band", "grid", None), P())
    return jax.shard_map(
        body, mesh=mesh, in_specs=placed, out_specs=P("band", "grid", None), check_vma=False
    )
```

```python
import functools
import math

import jax
import jax.numpy as jnp
import numpy as np
from jax import lax
from jax.experimental import pallas as pl
from jax.experimental.pallas import tpu as pltpu
from jax.sharding import PartitionSpec as P

box_length = 12.0
screening = 0.106
BF16 = jnp.bfloat16
F32 = jnp.float32
LANES = 256
HALF = 128
PACK = 3


def cas_table(length):
    points = np.arange(length)
    products = points[:, None] * points[None, :] % length
    phase = products.astype(np.float32) * np.float32(2.0 * math.pi / length)
    return (np.cos(phase) + np.sin(phase)).astype(BF16)


def screened_kernel(length):
    points = np.arange(length)
    folded = np.minimum(points, length - points).astype(np.float32)
    squares = folded * folded
    factor = np.float32((2.0 * math.pi / box_length) ** 2)
    wave_sq = factor * (squares[:, None, None] + squares[None, :, None] + squares[None, None, :])
    positive = np.where(wave_sq > 0.0, wave_sq, np.float32(1.0))
    screen = np.float32(4.0 * math.pi) * (
        np.float32(1.0) - np.exp(-positive / np.float32(4.0 * screening * screening))
    )
    screen = screen / positive / np.float32(length**3)
    return np.where(wave_sq > 0.0, screen, np.float32(0.0)).astype(np.float32)


def padded(array, width):
    return np.pad(array, [(0, 0)] * (array.ndim - 1) + [(0, width - array.shape[-1])])


def pack_body(in_ref, out_ref, rows, *, side):
    planes, bands = in_ref.shape[:2]
    pitch = rows.shape[0] // (planes * bands)
    for x in range(planes):
        values = in_ref[x].astype(F32)
        for y in range(side):
            part = values[:, y * side : (y + 1) * side]
            rows[pl.ds(x * bands * pitch + y, bands, stride=pitch), pl.ds(0, side)] = part
    pad = jnp.zeros((2 * side, LANES - PACK * side), BF16)
    for band in range(bands):
        parts = []
        for s in range(PACK):
            starts = [((PACK * e + s) * bands + band) * pitch for e in range(2)]
            both = [rows[pl.ds(start, side), :][:, :side] for start in starts]
            parts.append(jnp.concatenate(both, axis=0).astype(BF16))
        out_ref[band, 0] = jnp.concatenate(parts + [pad], axis=1)


def pack(orbitals, side):
    count, slab, plane = orbitals.shape
    steps = slab // (2 * PACK)
    return pl.pallas_call(
        functools.partial(pack_body, side=side),
        grid=(steps,),
        in_specs=[pl.BlockSpec((2 * PACK, count, plane), lambda m: (m, 0, 0))],
        out_specs=pl.BlockSpec((count, 1, 2 * side, LANES), lambda m: (0, m, 0, 0)),
        out_shape=jax.ShapeDtypeStruct((count, steps, 2 * side, LANES), BF16),
        scratch_shapes=[pltpu.VMEM((2 * PACK * count * (side + 4), HALF), F32)],
        compiler_params=pltpu.CompilerParams(vmem_limit_bytes=32 * 2**20),
    )(orbitals.transpose(1, 0, 2))


def unpack_body(level_ref, *refs, side, levels):
    pieces, (out_ref, rows) = refs[:-2], refs[-2:]
    planes, bands = out_ref.shape[:2]
    share = bands // levels
    pitch = rows.shape[0] // (planes * bands)
    for k, piece in enumerate(pieces):
        band = (level_ref[0] + k % levels) % levels * share + k // levels
        value = piece[0, 0].astype(F32)
        for s in range(PACK):
            part = value[:, s * side : (s + 1) * side]
            for e in range(2):
                start = ((PACK * e + s) * bands + band) * pitch
                rows[pl.ds(start, side), pl.ds(0, side)] = part[e * side : (e + 1) * side]
    for x in range(planes):
        parts = [rows[pl.ds(x * bands * pitch + y, bands, stride=pitch), :] for y in range(side)]
        out_ref[x] = jnp.concatenate([v[:, :side] for v in parts], axis=1)


def unpack(pieces, level, side, share):
    levels = len(pieces) // share
    bands = len(pieces)
    steps = pieces[0].shape[1]
    grid_spec = pltpu.PrefetchScalarGridSpec(
        num_scalar_prefetch=1,
        grid=(steps,),
        in_specs=[pl.BlockSpec((1, 1, 2 * side, LANES), lambda m, first: (0, m, 0, 0))] * bands,
        out_specs=pl.BlockSpec((2 * PACK, bands, side * side), lambda m, first: (m, 0, 0)),
        scratch_shapes=[pltpu.VMEM((2 * PACK * bands * (side + 4), HALF), F32)],
    )
    field = pl.pallas_call(
        functools.partial(unpack_body, side=side, levels=levels),
        grid_spec=grid_spec,
        out_shape=jax.ShapeDtypeStruct((2 * PACK * steps, bands, side * side), F32),
        compiler_params=pltpu.CompilerParams(vmem_limit_bytes=32 * 2**20),
    )(jnp.reshape(level, (1,)), *pieces)
    return field.transpose(1, 0, 2)


def dot(left, right):
    return lax.dot_general(left, right, (((1,), (0,)), ((), ())), preferred_element_type=F32)


def swap_thirds(values, side):
    pad = jnp.zeros((values[0].shape[0], LANES - PACK * side), values[0].dtype)
    return [
        jnp.concatenate([v[:, side * s : side * s + side] for v in values] + [pad], axis=1)
        for s in range(PACK)
    ]


def solve_body(*refs, side, pitch, places, pieces, count, has_start, cuts):
    own_pieces, rest = refs[:pieces], refs[pieces:]
    arrays = rest[: max(a for a, _ in places) + 1]
    rest = rest[len(arrays) :]
    if has_start:
        start_hbm, rest = rest[0], rest[1:]
    kernel_hbm, cas2_ref, ahead_ref, back_ref, thirds_ref = rest[:5]
    out_refs = rest[5 : 5 + max(cuts, 1)]
    own_ref, bands, kernel_ref, low, high, own_sem, band_sem, wide_sem, *totals = rest[5 + len(out_refs) :]
    total_ref = totals[0] if totals else out_refs[0]
    steps = own_ref.shape[0]
    half = side // 2
    part = steps // pieces

    own_copies = [
        pltpu.make_async_copy(ref.at[0], own_ref.at[pl.ds(k * part, part)], own_sem.at[k])
        for k, ref in enumerate(own_pieces)
    ]
    band_copies = [
        pltpu.make_async_copy(arrays[a].at[k], bands.at[j], band_sem.at[j])
        for j, (a, k) in enumerate(places)
    ]
    kernel_copy = pltpu.make_async_copy(kernel_hbm, kernel_ref, wide_sem.at[0])
    for copy in own_copies + band_copies[:PACK]:
        copy.start()
    if not has_start:
        total_ref[...] = jnp.zeros_like(total_ref)
    for j in range(len(places), bands.shape[0]):
        bands[j] = jnp.zeros_like(bands[j])

    def put(plane, value):
        low[pl.ds(plane * pitch, side), :] = value[:, :HALF]
        high[pl.ds(plane * pitch, side), :] = value[:, HALF:]

    def get(plane):
        parts = [r[pl.ds(plane * pitch, side), :] for r in (low, high)]
        return jnp.concatenate(parts, axis=1)

    def put_across(row, value):
        low[pl.ds(row, side, stride=pitch), :] = value[:, :HALF]
        high[pl.ds(row, side, stride=pitch), :] = value[:, HALF:]

    def get_across(row):
        parts = [r[pl.ds(row, side, stride=pitch), :] for r in (low, high)]
        return jnp.concatenate(parts, axis=1)

    def first_two(base, work):
        sources = []
        for step in work:
            density = [own_ref[step] * bands[base + k, step] for k in range(PACK)]
            sources += [(6 * step + s, v) for s, v in enumerate(swap_thirds(density, side))]
        along_z = [dot(v, thirds_ref[...]).astype(BF16) for _, v in sources]
        along_y = [dot(cas2_ref[...], v) for v in along_z]
        for (plane, _), v in zip(sources, along_y):
            put(plane, v[:side])
            put(plane + PACK, v[side:])

    def middle_two(rows):
        planes = [
            jnp.concatenate([get_across(2 * r), get_across(2 * r + 1)], axis=0).astype(BF16)
            for r in rows
        ]
        waves = [dot(ahead_ref[...], v) for v in planes]
        waves = [(v * kernel_ref[r]).astype(BF16) for r, v in zip(rows, waves)]
        planes = [dot(back_ref[...], v) for v in waves]
        for r, v in zip(rows, planes):
            put_across(2 * r, v[:side])
            put_across(2 * r + 1, v[side:])

    def last_two(base, work):
        halves = [
            [
                jnp.concatenate([get(6 * t + s), get(6 * t + PACK + s)], axis=0).astype(BF16)
                for s in range(PACK)
            ]
            for t in work
        ]
        along_y = [[dot(cas2_ref[...], v).astype(BF16) for v in vs] for vs in halves]
        swapped = [swap_thirds(vs, side) for vs in along_y]
        potential = [[dot(v, thirds_ref[...]) for v in vs] for vs in swapped]
        for t, vs in zip(work, potential):
            terms = [v * bands[base + k, t].astype(F32) for k, v in enumerate(vs)]
            total_ref[t] += terms[0] + terms[1] + terms[2]

    def loop(count, at_once, run):
        if at_once >= count:
            run(list(range(count)))
        else:
            lax.fori_loop(
                0, count // at_once, lambda q, c: run([q * at_once + w for w in range(at_once)]) or c, 0
            )

    for copy in own_copies + band_copies[:PACK]:
        copy.wait()
    kernel_copy.start()
    if has_start:
        start_copy = pltpu.make_async_copy(start_hbm, total_ref, wide_sem.at[1])
        start_copy.start()
    for copy in band_copies[PACK:]:
        copy.start()

    def group(g, carry):
        base = g * PACK
        for k in range(PACK):

            @pl.when((g > 0) & (base + k < len(places)))
            def _(k=k):
                pltpu.make_async_copy(
                    arrays[0].at[0], bands.at[base + k], band_sem.at[base + k]
                ).wait()
        loop(steps, at_once[0] or steps, lambda work: first_two(base, work))

        @pl.when(g == 0)
        def _():
            kernel_copy.wait()
            if has_start:
                start_copy.wait()

        loop(half, at_once[1] or half, middle_two)
        loop(steps, at_once[2] or steps, lambda work: last_two(base, work))
        return carry

    lax.fori_loop(0, count, group, 0)
    if totals:
        for k, out_ref in enumerate(out_refs):
            size = out_ref.shape[1]
            out_ref[0] = total_ref[k * size : (k + 1) * size].astype(out_ref.dtype)


at_once = (0, 0, 0)


def solve(own, bands, start, tables, side, cuts=0):
    places = [(a, k) for a, array in enumerate(bands) for k in range(array.shape[0])]
    part = own[0].shape[1]
    shape = (part * len(own),) + own[0].shape[2:]
    pitch = side + 4
    count = -(-len(places) // PACK)
    vmem = pl.BlockSpec(memory_space=pltpu.VMEM)
    hbm = pl.BlockSpec(memory_space=pl.ANY)
    first = [*own, *bands] + ([] if start is None else [start]) + [tables[0]]
    body = functools.partial(
        solve_body, side=side, pitch=pitch, places=places, pieces=len(own), count=count,
        has_start=start is not None, cuts=cuts
    )
    scratch = [
        pltpu.VMEM(shape, BF16),
        pltpu.VMEM((count * PACK,) + shape, BF16),
        pltpu.VMEM(tables[0].shape, F32),
        pltpu.VMEM((side * pitch, HALF), F32),
        pltpu.VMEM((side * pitch, HALF), F32),
        pltpu.SemaphoreType.DMA((len(own),)),
        pltpu.SemaphoreType.DMA((count * PACK,)),
        pltpu.SemaphoreType.DMA((2,)),
    ]
    piece = jax.ShapeDtypeStruct((1, shape[0] // max(cuts, 1)) + shape[1:], BF16)
    return pl.pallas_call(
        body,
        in_specs=[hbm] * len(first) + [vmem] * 4,
        out_specs=[vmem] * cuts if cuts else vmem,
        out_shape=[piece] * cuts if cuts else jax.ShapeDtypeStruct(shape, F32),
        scratch_shapes=scratch + ([pltpu.VMEM(shape, F32)] if cuts else []),
        compiler_params=pltpu.CompilerParams(vmem_limit_bytes=60 * 2**20),
        cost_estimate=pl.CostEstimate(
            flops=len(places) * 96 * side**4, bytes_accessed=10 * 2**20, transcendentals=0
        ),
    )(*first, *tables[1:])


def make_tables(side, slab, level):
    cas = cas_table(side)
    two = np.eye(2, dtype=np.float32)
    cas2 = jnp.asarray(np.kron(two, cas.astype(np.float32)).astype(BF16))
    three = np.kron(np.eye(PACK, dtype=np.float32), cas.astype(np.float32))
    margin = LANES - three.shape[0]
    thirds = jnp.asarray(np.pad(three, ((0, margin), (0, margin))).astype(BF16))
    screen = screened_kernel(side).transpose(1, 0, 2)
    screen = padded(np.concatenate([screen] * PACK, axis=-1), LANES)
    screen = jnp.asarray(screen.reshape(side // 2, 2 * side, LANES))
    table = jnp.asarray(cas)
    moved = lax.dynamic_slice_in_dim(jnp.concatenate([table, table], 0), level * slab, side, 0)
    zero = jnp.zeros_like(moved)
    back = jnp.concatenate(
        [jnp.concatenate([moved, zero], 1), jnp.concatenate([zero, moved], 1)], 0
    )
    return screen, cas2, back.T, back, thirds


def from_level(value, ahead):
    count = lax.axis_size("grid")
    pairs = [((h + ahead) % count, h) for h in range(count)]
    return lax.ppermute(value, "grid", pairs)


def flip(value, bit):
    return lax.ppermute(value, "band", [(b, b ^ bit) for b in range(lax.axis_size("band"))])


def pick(options, index):
    result = options[0]
    for k in range(1, len(options)):
        result = jnp.where(index == k, options[k], result)
    return result


def own_slabs(packed, per_device, which):
    levels = lax.axis_size("grid")
    level = lax.axis_index("grid")
    pieces = []
    for ahead in range(levels):
        start = (level + levels - ahead) % levels * per_device + which
        piece = lax.dynamic_slice_in_dim(packed, start, 1, 0)
        pieces.append(from_level(piece, ahead) if ahead else piece)
    return pieces


def whole(slab):
    levels = lax.axis_size("grid")
    pieces = [slab] + [from_level(slab, ahead) for ahead in range(1, levels)]
    return jnp.concatenate(pieces, axis=1)


def after(value, *others):
    return lax.optimization_barrier((value, others))[0]


def share_out(packed, owners, which):
    band = lax.axis_index("band")
    core, line = band % 2, band // 2
    share = packed.shape[0] // 4
    parts = []
    for k in range(4):
        part = lax.dynamic_slice_in_dim(packed, (line ^ k) * share + which, 1, 0)
        parts.append(flip(part, 2 * k) if k else part)
    here, there = owners[core], owners[1 - core]
    mine = pick(parts, line ^ (here // 2))
    other = flip(pick(parts, line ^ (there // 2)), 1)
    return jnp.where(here % 2 == core, mine, other), parts


def fields_small(packed, owners, tables, side):
    levels = lax.axis_size("grid")
    own0 = own_slabs(packed, 2, 0)
    slab0, parts = share_out(packed, owners, 0)
    slab1, _ = share_out(after(packed, parts), owners, 1)
    slab0, own0 = lax.optimization_barrier((slab0, own0))
    mine0 = whole(slab0)
    x0, y0 = flip(mine0, 2), flip(mine0, 4)
    mine1 = whole(after(slab1, mine0))
    own1 = own_slabs(after(packed, mine1), 2, 1)
    late = after(mine1, x0, y0)
    x1, y1 = flip(late, 2), flip(late, 4)
    near = [mine0, mine1, x0, y0]
    near = near + [flip(v, 1) for v in near]
    total0 = solve(own0, near, None, tables, side)
    x1, y1, total0 = lax.optimization_barrier((x1, y1, total0))
    corner = [flip(after(x0, x1, y1), 4), flip(y1, 2)]
    far = [x1, y1, flip(x1, 1), flip(y1, 1)]
    total1 = solve(own1, near, None, tables, side)
    corner, total1 = lax.optimization_barrier((corner, total1))
    far = far + corner + [flip(v, 1) for v in corner]
    field0 = solve(own0, far, total0, tables, side, levels)
    field1 = solve(own1, far, total1, tables, side, levels)
    return [field0, field1]


def fields_any(packed, owners, tables, side):
    band = lax.axis_index("band")
    levels = lax.axis_size("grid")
    per_device = packed.shape[0] // levels
    own = [own_slabs(packed, per_device, i) for i in range(per_device)]
    totals = [None] * per_device
    for r in range(owners.shape[0]):
        kept = jnp.where(band == owners[r], packed, jnp.zeros_like(packed))
        bands = whole(lax.psum(kept, "band"))
        cuts = levels if r == owners.shape[0] - 1 else 0
        totals = [solve(o, [bands], t, tables, side, cuts) for o, t in zip(own, totals)]
    return totals


def body(orbitals, owners):
    band_count, slab, plane = orbitals.shape
    levels = lax.axis_size("grid")
    level = lax.axis_index("grid")
    side = slab * levels
    tables = make_tables(side, slab, level)
    packed = pack(orbitals, side)
    small = (lax.axis_size("band"), owners.shape[0], band_count, levels) == (8, 2, 8, 4)
    fields = (fields_small if small else fields_any)(packed, owners, tables, side)
    pieces = []
    for field in fields:
        for ahead in range(levels):
            piece = field[(levels - ahead) % levels]
            pieces.append(from_level(piece, ahead) if ahead else piece)
    return unpack(pieces, level, side, len(fields))


def solution(mesh):
    placed = (P("band", "grid", None), P())
    return jax.shard_map(
        body, mesh=mesh, in_specs=placed, out_specs=P("band", "grid", None), check_vma=False
    )
```

```python
import functools
import math

import jax
import jax.numpy as jnp
import numpy as np
from jax import lax
from jax.experimental import pallas as pl
from jax.experimental.pallas import tpu as pltpu
from jax.sharding import PartitionSpec as P

box_length = 12.0
screening = 0.106
BF16 = jnp.bfloat16
F32 = jnp.float32
LANES = 256
HALF = 128
PACK = 3


def cas_table(length):
    points = np.arange(length)
    products = points[:, None] * points[None, :] % length
    phase = products.astype(np.float32) * np.float32(2.0 * math.pi / length)
    return (np.cos(phase) + np.sin(phase)).astype(BF16)


def screened_kernel(length):
    points = np.arange(length)
    folded = np.minimum(points, length - points).astype(np.float32)
    squares = folded * folded
    factor = np.float32((2.0 * math.pi / box_length) ** 2)
    wave_sq = factor * (squares[:, None, None] + squares[None, :, None] + squares[None, None, :])
    positive = np.where(wave_sq > 0.0, wave_sq, np.float32(1.0))
    screen = np.float32(4.0 * math.pi) * (
        np.float32(1.0) - np.exp(-positive / np.float32(4.0 * screening * screening))
    )
    screen = screen / positive / np.float32(length**3)
    return np.where(wave_sq > 0.0, screen, np.float32(0.0)).astype(np.float32)


def padded(array, width):
    return np.pad(array, [(0, 0)] * (array.ndim - 1) + [(0, width - array.shape[-1])])


def pack_body(in_ref, out_ref, rows, *, side):
    planes, bands = in_ref.shape[:2]
    pitch = rows.shape[0] // (planes * bands)
    for x in range(planes):
        values = in_ref[x].astype(F32)
        for y in range(side):
            part = values[:, y * side : (y + 1) * side]
            rows[pl.ds(x * bands * pitch + y, bands, stride=pitch), pl.ds(0, side)] = part
    pad = jnp.zeros((2 * side, LANES - PACK * side), BF16)
    for band in range(bands):
        parts = []
        for s in range(PACK):
            starts = [((PACK * e + s) * bands + band) * pitch for e in range(2)]
            both = [rows[pl.ds(start, side), :][:, :side] for start in starts]
            parts.append(jnp.concatenate(both, axis=0).astype(BF16))
        out_ref[band, 0] = jnp.concatenate(parts + [pad], axis=1)


def pack(orbitals, side):
    count, slab, plane = orbitals.shape
    steps = slab // (2 * PACK)
    return pl.pallas_call(
        functools.partial(pack_body, side=side),
        grid=(steps,),
        in_specs=[pl.BlockSpec((2 * PACK, count, plane), lambda m: (m, 0, 0))],
        out_specs=pl.BlockSpec((count, 1, 2 * side, LANES), lambda m: (0, m, 0, 0)),
        out_shape=jax.ShapeDtypeStruct((count, steps, 2 * side, LANES), BF16),
        scratch_shapes=[pltpu.VMEM((2 * PACK * count * (side + 4), HALF), F32)],
        compiler_params=pltpu.CompilerParams(vmem_limit_bytes=32 * 2**20),
    )(orbitals.transpose(1, 0, 2))


def unpack_body(level_ref, *refs, side, levels):
    pieces, (out_ref, rows) = refs[:-2], refs[-2:]
    planes, bands = out_ref.shape[:2]
    share = bands // levels
    pitch = rows.shape[0] // (planes * bands)
    for k, piece in enumerate(pieces):
        band = (level_ref[0] + k % levels) % levels * share + k // levels
        value = piece[0, 0].astype(F32)
        for s in range(PACK):
            part = value[:, s * side : (s + 1) * side]
            for e in range(2):
                start = ((PACK * e + s) * bands + band) * pitch
                rows[pl.ds(start, side), pl.ds(0, side)] = part[e * side : (e + 1) * side]
    for x in range(planes):
        parts = [rows[pl.ds(x * bands * pitch + y, bands, stride=pitch), :] for y in range(side)]
        out_ref[x] = jnp.concatenate([v[:, :side] for v in parts], axis=1)


def unpack(pieces, level, side, share):
    levels = len(pieces) // share
    bands = len(pieces)
    steps = pieces[0].shape[1]
    grid_spec = pltpu.PrefetchScalarGridSpec(
        num_scalar_prefetch=1,
        grid=(steps,),
        in_specs=[pl.BlockSpec((1, 1, 2 * side, LANES), lambda m, first: (0, m, 0, 0))] * bands,
        out_specs=pl.BlockSpec((2 * PACK, bands, side * side), lambda m, first: (m, 0, 0)),
        scratch_shapes=[pltpu.VMEM((2 * PACK * bands * (side + 4), HALF), F32)],
    )
    field = pl.pallas_call(
        functools.partial(unpack_body, side=side, levels=levels),
        grid_spec=grid_spec,
        out_shape=jax.ShapeDtypeStruct((2 * PACK * steps, bands, side * side), F32),
        compiler_params=pltpu.CompilerParams(vmem_limit_bytes=32 * 2**20),
    )(jnp.reshape(level, (1,)), *pieces)
    return field.transpose(1, 0, 2)


def dot(left, right):
    return lax.dot_general(left, right, (((1,), (0,)), ((), ())), preferred_element_type=F32)


def swap_thirds(values, side):
    pad = jnp.zeros((values[0].shape[0], LANES - PACK * side), values[0].dtype)
    return [
        jnp.concatenate([v[:, side * s : side * s + side] for v in values] + [pad], axis=1)
        for s in range(PACK)
    ]


def solve_body(*refs, side, pitch, places, pieces, count, has_start, cuts):
    own_pieces, rest = refs[:pieces], refs[pieces:]
    arrays = rest[: max(a for a, _ in places) + 1]
    rest = rest[len(arrays) :]
    if has_start:
        start_hbm, rest = rest[0], rest[1:]
    kernel_hbm, cas2_ref, ahead_ref, back_ref, thirds_ref = rest[:5]
    out_refs = rest[5 : 5 + max(cuts, 1)]
    own_ref, bands, kernel_ref, low, high, own_sem, band_sem, wide_sem, *totals = rest[5 + len(out_refs) :]
    total_ref = totals[0] if totals else out_refs[0]
    steps = own_ref.shape[0]
    half = side // 2
    part = steps // pieces

    own_copies = [
        pltpu.make_async_copy(ref.at[0], own_ref.at[pl.ds(k * part, part)], own_sem.at[k])
        for k, ref in enumerate(own_pieces)
    ]
    band_copies = [
        pltpu.make_async_copy(arrays[a].at[k], bands.at[j], band_sem.at[j])
        for j, (a, k) in enumerate(places)
    ]
    kernel_copy = pltpu.make_async_copy(kernel_hbm, kernel_ref, wide_sem.at[0])
    for copy in own_copies + band_copies[:PACK]:
        copy.start()
    if not has_start:
        total_ref[...] = jnp.zeros_like(total_ref)
    for j in range(len(places), bands.shape[0]):
        bands[j] = jnp.zeros_like(bands[j])

    def put(plane, value):
        low[pl.ds(plane * pitch, side), :] = value[:, :HALF]
        high[pl.ds(plane * pitch, side), :] = value[:, HALF:]

    def get(plane):
        parts = [r[pl.ds(plane * pitch, side), :] for r in (low, high)]
        return jnp.concatenate(parts, axis=1)

    def put_across(row, value):
        low[pl.ds(row, side, stride=pitch), :] = value[:, :HALF]
        high[pl.ds(row, side, stride=pitch), :] = value[:, HALF:]

    def get_across(row):
        parts = [r[pl.ds(row, side, stride=pitch), :] for r in (low, high)]
        return jnp.concatenate(parts, axis=1)

    def first_two(base, work):
        sources = []
        for step in work:
            density = [own_ref[step] * bands[base + k, step] for k in range(PACK)]
            sources += [(6 * step + s, v) for s, v in enumerate(swap_thirds(density, side))]
        along_z = [dot(v, thirds_ref[...]).astype(BF16) for _, v in sources]
        along_y = [dot(cas2_ref[...], v) for v in along_z]
        for (plane, _), v in zip(sources, along_y):
            put(plane, v[:side])
            put(plane + PACK, v[side:])

    def screen(r):
        both = [kernel_ref[min(b, side - b)] for b in (2 * r, 2 * r + 1)]
        return jnp.concatenate(both, axis=0)

    def middle_two(rows):
        planes = [
            jnp.concatenate([get_across(2 * r), get_across(2 * r + 1)], axis=0).astype(BF16)
            for r in rows
        ]
        waves = [dot(ahead_ref[...], v) for v in planes]
        waves = [(v * screen(r)).astype(BF16) for r, v in zip(rows, waves)]
        planes = [dot(back_ref[...], v) for v in waves]
        for r, v in zip(rows, planes):
            put_across(2 * r, v[:side])
            put_across(2 * r + 1, v[side:])

    def last_two(base, work):
        halves = [
            [
                jnp.concatenate([get(6 * t + s), get(6 * t + PACK + s)], axis=0).astype(BF16)
                for s in range(PACK)
            ]
            for t in work
        ]
        along_y = [[dot(cas2_ref[...], v).astype(BF16) for v in vs] for vs in halves]
        swapped = [swap_thirds(vs, side) for vs in along_y]
        potential = [[dot(v, thirds_ref[...]) for v in vs] for vs in swapped]
        for t, vs in zip(work, potential):
            terms = [v * bands[base + k, t].astype(F32) for k, v in enumerate(vs)]
            total_ref[t] += terms[0] + terms[1] + terms[2]

    for copy in own_copies + band_copies[:PACK]:
        copy.wait()
    kernel_copy.start()
    if has_start:
        start_copy = pltpu.make_async_copy(start_hbm, total_ref, wide_sem.at[1])
        start_copy.start()
    for copy in band_copies[PACK:]:
        copy.start()

    def group(g, carry):
        base = g * PACK
        for k in range(PACK):

            @pl.when((g > 0) & (base + k < len(places)))
            def _(k=k):
                pltpu.make_async_copy(
                    arrays[0].at[0], bands.at[base + k], band_sem.at[base + k]
                ).wait()
        first_two(base, list(range(steps)))

        @pl.when(g == 0)
        def _():
            kernel_copy.wait()
            if has_start:
                start_copy.wait()

        middle_two(list(range(half)))
        last_two(base, list(range(steps)))
        return carry

    lax.fori_loop(0, count, group, 0)
    if totals:
        for k, out_ref in enumerate(out_refs):
            size = out_ref.shape[1]
            out_ref[0] = total_ref[k * size : (k + 1) * size].astype(out_ref.dtype)


def solve(own, bands, start, tables, side, cuts=0):
    places = [(a, k) for a, array in enumerate(bands) for k in range(array.shape[0])]
    part = own[0].shape[1]
    shape = (part * len(own),) + own[0].shape[2:]
    pitch = side + 4
    count = -(-len(places) // PACK)
    vmem = pl.BlockSpec(memory_space=pltpu.VMEM)
    hbm = pl.BlockSpec(memory_space=pl.ANY)
    first = [*own, *bands] + ([] if start is None else [start]) + [tables[0]]
    body = functools.partial(
        solve_body, side=side, pitch=pitch, places=places, pieces=len(own), count=count,
        has_start=start is not None, cuts=cuts
    )
    scratch = [
        pltpu.VMEM(shape, BF16),
        pltpu.VMEM((count * PACK,) + shape, BF16),
        pltpu.VMEM(tables[0].shape, F32),
        pltpu.VMEM((side * pitch, HALF), F32),
        pltpu.VMEM((side * pitch, HALF), F32),
        pltpu.SemaphoreType.DMA((len(own),)),
        pltpu.SemaphoreType.DMA((count * PACK,)),
        pltpu.SemaphoreType.DMA((2,)),
    ]
    piece = jax.ShapeDtypeStruct((1, shape[0] // max(cuts, 1)) + shape[1:], BF16)
    return pl.pallas_call(
        body,
        in_specs=[hbm] * len(first) + [vmem] * 4,
        out_specs=[vmem] * cuts if cuts else vmem,
        out_shape=[piece] * cuts if cuts else jax.ShapeDtypeStruct(shape, F32),
        scratch_shapes=scratch + ([pltpu.VMEM(shape, F32)] if cuts else []),
        compiler_params=pltpu.CompilerParams(vmem_limit_bytes=60 * 2**20),
        cost_estimate=pl.CostEstimate(
            flops=len(places) * 96 * side**4, bytes_accessed=10 * 2**20, transcendentals=0
        ),
    )(*first, *tables[1:])


def make_tables(side, slab, level):
    cas = cas_table(side)
    two = np.eye(2, dtype=np.float32)
    cas2 = jnp.asarray(np.kron(two, cas.astype(np.float32)).astype(BF16))
    three = np.kron(np.eye(PACK, dtype=np.float32), cas.astype(np.float32))
    margin = LANES - three.shape[0]
    thirds = jnp.asarray(np.pad(three, ((0, margin), (0, margin))).astype(BF16))
    screen = screened_kernel(side)[: side // 2 + 1]
    screen = padded(np.concatenate([screen] * PACK, axis=-1), LANES)
    screen = jnp.asarray(screen)
    table = jnp.asarray(cas)
    moved = lax.dynamic_slice_in_dim(jnp.concatenate([table, table], 0), level * slab, side, 0)
    zero = jnp.zeros_like(moved)
    back = jnp.concatenate(
        [jnp.concatenate([moved, zero], 1), jnp.concatenate([zero, moved], 1)], 0
    )
    return screen, cas2, back.T, back, thirds


def from_level(value, ahead):
    count = lax.axis_size("grid")
    pairs = [((h + ahead) % count, h) for h in range(count)]
    return lax.ppermute(value, "grid", pairs)


def flip(value, bit):
    return lax.ppermute(value, "band", [(b, b ^ bit) for b in range(lax.axis_size("band"))])


def pick(options, index):
    result = options[0]
    for k in range(1, len(options)):
        result = jnp.where(index == k, options[k], result)
    return result


def own_slabs(packed, per_device, which):
    levels = lax.axis_size("grid")
    level = lax.axis_index("grid")
    pieces = []
    for ahead in range(levels):
        start = (level + levels - ahead) % levels * per_device + which
        piece = lax.dynamic_slice_in_dim(packed, start, 1, 0)
        pieces.append(from_level(piece, ahead) if ahead else piece)
    return pieces


def whole(slab):
    levels = lax.axis_size("grid")
    pieces = [slab] + [from_level(slab, ahead) for ahead in range(1, levels)]
    return jnp.concatenate(pieces, axis=1)


def after(value, *others):
    return lax.optimization_barrier((value, others))[0]


def hand_out(packed, which):
    line = lax.axis_index("band") // 2
    share = packed.shape[0] // 4
    parts = []
    for k in range(4):
        part = lax.dynamic_slice_in_dim(packed, (line ^ k) * share + which, 1, 0)
        parts.append(flip(part, 2 * k) if k else part)
    return parts


def keep(parts, owners):
    band = lax.axis_index("band")
    core, line = band % 2, band // 2
    here, there = owners[core], owners[1 - core]
    mine = pick(parts, line ^ (here // 2))
    other = flip(pick(parts, line ^ (there // 2)), 1)
    return jnp.where(here % 2 == core, mine, other)


def fields_small(packed, owners, tables, side):
    levels = lax.axis_size("grid")
    own0 = own_slabs(packed, 2, 0)
    parts0, own0 = lax.optimization_barrier((hand_out(packed, 0), own0))
    slab0 = keep(parts0, owners)
    slab1 = keep(hand_out(after(packed, parts0), 1), owners)
    slab0, tables = lax.optimization_barrier((slab0, tables))
    mine0 = whole(slab0)
    x0, y0 = flip(mine0, 2), flip(mine0, 4)
    mine1 = whole(after(slab1, mine0))
    own1 = own_slabs(after(packed, mine1), 2, 1)
    late = after(mine1, x0, y0)
    x1, y1 = flip(late, 2), flip(late, 4)
    near = [mine0, mine1, x0, y0]
    near = near + [flip(v, 1) for v in near]
    total0 = solve(own0, near, None, tables, side)
    x1, y1, total0 = lax.optimization_barrier((x1, y1, total0))
    corner = [flip(after(x0, x1, y1), 4), flip(y1, 2)]
    far = [x1, y1, flip(x1, 1), flip(y1, 1)]
    total1 = solve(own1, near, None, tables, side)
    corner, total1 = lax.optimization_barrier((corner, total1))
    far = far + corner + [flip(v, 1) for v in corner]
    field0 = solve(own0, far, total0, tables, side, levels)
    field1 = solve(own1, far, total1, tables, side, levels)
    return [field0, field1]


def fields_any(packed, owners, tables, side):
    band = lax.axis_index("band")
    levels = lax.axis_size("grid")
    per_device = packed.shape[0] // levels
    own = [own_slabs(packed, per_device, i) for i in range(per_device)]
    totals = [None] * per_device
    for r in range(owners.shape[0]):
        kept = jnp.where(band == owners[r], packed, jnp.zeros_like(packed))
        bands = whole(lax.psum(kept, "band"))
        cuts = levels if r == owners.shape[0] - 1 else 0
        totals = [solve(o, [bands], t, tables, side, cuts) for o, t in zip(own, totals)]
    return totals


def body(orbitals, owners):
    band_count, slab, plane = orbitals.shape
    levels = lax.axis_size("grid")
    level = lax.axis_index("grid")
    side = slab * levels
    tables = make_tables(side, slab, level)
    packed = pack(orbitals, side)
    small = (lax.axis_size("band"), owners.shape[0], band_count, levels) == (8, 2, 8, 4)
    fields = (fields_small if small else fields_any)(packed, owners, tables, side)
    pieces = []
    for field in fields:
        for ahead in range(levels):
            piece = field[(levels - ahead) % levels]
            pieces.append(from_level(piece, ahead) if ahead else piece)
    return unpack(pieces, level, side, len(fields))


def solution(mesh):
    placed = (P("band", "grid", None), P())
    return jax.shard_map(
        body, mesh=mesh, in_specs=placed, out_specs=P("band", "grid", None), check_vma=False
    )
```

```python
import functools
import math

import jax
import jax.numpy as jnp
import numpy as np
from jax import lax
from jax.experimental import pallas as pl
from jax.experimental.pallas import tpu as pltpu
from jax.sharding import PartitionSpec as P

box_length = 12.0
screening = 0.106
BF16 = jnp.bfloat16
F32 = jnp.float32
LANES = 256
HALF = 128
PACK = 3


def cas_table(length):
    points = np.arange(length)
    products = points[:, None] * points[None, :] % length
    phase = products.astype(np.float32) * np.float32(2.0 * math.pi / length)
    return (np.cos(phase) + np.sin(phase)).astype(BF16)


def screened_kernel(length):
    points = np.arange(length)
    folded = np.minimum(points, length - points).astype(np.float32)
    squares = folded * folded
    factor = np.float32((2.0 * math.pi / box_length) ** 2)
    wave_sq = factor * (squares[:, None, None] + squares[None, :, None] + squares[None, None, :])
    positive = np.where(wave_sq > 0.0, wave_sq, np.float32(1.0))
    screen = np.float32(4.0 * math.pi) * (
        np.float32(1.0) - np.exp(-positive / np.float32(4.0 * screening * screening))
    )
    screen = screen / positive / np.float32(length**3)
    return np.where(wave_sq > 0.0, screen, np.float32(0.0)).astype(np.float32)


def padded(array, width):
    return np.pad(array, [(0, 0)] * (array.ndim - 1) + [(0, width - array.shape[-1])])


def pack_body(in_ref, out_ref, rows, *, side):
    planes, bands = in_ref.shape[:2]
    pitch = rows.shape[0] // (planes * bands)
    for x in range(planes):
        values = in_ref[x].astype(F32)
        for y in range(side):
            part = values[:, y * side : (y + 1) * side]
            rows[pl.ds(x * bands * pitch + y, bands, stride=pitch), pl.ds(0, side)] = part
    pad = jnp.zeros((2 * side, LANES - PACK * side), BF16)
    for band in range(bands):
        parts = []
        for s in range(PACK):
            starts = [((PACK * e + s) * bands + band) * pitch for e in range(2)]
            both = [rows[pl.ds(start, side), :][:, :side] for start in starts]
            parts.append(jnp.concatenate(both, axis=0).astype(BF16))
        out_ref[band, 0] = jnp.concatenate(parts + [pad], axis=1)


def pack(orbitals, side):
    count, slab, plane = orbitals.shape
    steps = slab // (2 * PACK)
    return pl.pallas_call(
        functools.partial(pack_body, side=side),
        grid=(steps,),
        in_specs=[pl.BlockSpec((2 * PACK, count, plane), lambda m: (m, 0, 0))],
        out_specs=pl.BlockSpec((count, 1, 2 * side, LANES), lambda m: (0, m, 0, 0)),
        out_shape=jax.ShapeDtypeStruct((count, steps, 2 * side, LANES), BF16),
        scratch_shapes=[pltpu.VMEM((2 * PACK * count * (side + 4), HALF), F32)],
        compiler_params=pltpu.CompilerParams(vmem_limit_bytes=32 * 2**20),
    )(orbitals.transpose(1, 0, 2))


def unpack_body(level_ref, *refs, side, levels):
    pieces, (out_ref, rows) = refs[:-2], refs[-2:]
    planes, bands = out_ref.shape[:2]
    share = bands // levels
    pitch = rows.shape[0] // (planes * bands)
    for k, piece in enumerate(pieces):
        band = (level_ref[0] + k % levels) % levels * share + k // levels
        value = piece[0, 0].astype(F32)
        for s in range(PACK):
            part = value[:, s * side : (s + 1) * side]
            for e in range(2):
                start = ((PACK * e + s) * bands + band) * pitch
                rows[pl.ds(start, side), pl.ds(0, side)] = part[e * side : (e + 1) * side]
    for x in range(planes):
        parts = [rows[pl.ds(x * bands * pitch + y, bands, stride=pitch), :] for y in range(side)]
        out_ref[x] = jnp.concatenate([v[:, :side] for v in parts], axis=1)


def unpack(pieces, level, side, share):
    levels = len(pieces) // share
    bands = len(pieces)
    steps = pieces[0].shape[1]
    grid_spec = pltpu.PrefetchScalarGridSpec(
        num_scalar_prefetch=1,
        grid=(steps,),
        in_specs=[pl.BlockSpec((1, 1, 2 * side, LANES), lambda m, first: (0, m, 0, 0))] * bands,
        out_specs=pl.BlockSpec((2 * PACK, bands, side * side), lambda m, first: (m, 0, 0)),
        scratch_shapes=[pltpu.VMEM((2 * PACK * bands * (side + 4), HALF), F32)],
    )
    field = pl.pallas_call(
        functools.partial(unpack_body, side=side, levels=levels),
        grid_spec=grid_spec,
        out_shape=jax.ShapeDtypeStruct((2 * PACK * steps, bands, side * side), F32),
        compiler_params=pltpu.CompilerParams(vmem_limit_bytes=32 * 2**20),
    )(jnp.reshape(level, (1,)), *pieces)
    return field.transpose(1, 0, 2)


def dot(left, right):
    return lax.dot_general(left, right, (((1,), (0,)), ((), ())), preferred_element_type=F32)


def swap_thirds(values, side):
    pad = jnp.zeros((values[0].shape[0], LANES - PACK * side), values[0].dtype)
    return [
        jnp.concatenate([v[:, side * s : side * s + side] for v in values] + [pad], axis=1)
        for s in range(PACK)
    ]


def solve_body(*refs, side, pitch, places, pieces, owns, count, has_start, cuts):
    own_pieces, rest = refs[: pieces * owns], refs[pieces * owns :]
    arrays = rest[: max(a for a, _ in places) + 1]
    rest = rest[len(arrays) :]
    starts, rest = rest[: owns * has_start], rest[owns * has_start :]
    kernel_hbm, cas2_ref, ahead_ref, back_ref, thirds_ref = rest[:5]
    out_refs = rest[5 : 4 + max(cuts, 1) + owns]
    own_ref, bands, kernel_ref, low, high, own_sem, band_sem, wide_sem, *totals = rest[5 + len(out_refs) :]
    total_ref = totals[0] if totals else out_refs[0]
    steps = own_ref.shape[1]
    half = side // 2
    part = steps // pieces

    own_copies = [
        pltpu.make_async_copy(
            ref.at[0], own_ref.at[k // pieces, pl.ds(k % pieces * part, part)], own_sem.at[k]
        )
        for k, ref in enumerate(own_pieces)
    ]
    band_copies = [
        pltpu.make_async_copy(arrays[a].at[k], bands.at[j], band_sem.at[j])
        for j, (a, k) in enumerate(places)
    ]
    kernel_copy = pltpu.make_async_copy(kernel_hbm, kernel_ref, wide_sem.at[0])
    for copy in own_copies + band_copies[:PACK]:
        copy.start()
    if not has_start:
        total_ref[...] = jnp.zeros_like(total_ref)
    for j in range(len(places), bands.shape[0]):
        bands[j] = jnp.zeros_like(bands[j])

    def put(plane, value):
        low[pl.ds(plane * pitch, side), :] = value[:, :HALF]
        high[pl.ds(plane * pitch, side), :] = value[:, HALF:]

    def get(plane):
        parts = [r[pl.ds(plane * pitch, side), :] for r in (low, high)]
        return jnp.concatenate(parts, axis=1)

    def put_across(row, value):
        low[pl.ds(row, side, stride=pitch), :] = value[:, :HALF]
        high[pl.ds(row, side, stride=pitch), :] = value[:, HALF:]

    def get_across(row):
        parts = [r[pl.ds(row, side, stride=pitch), :] for r in (low, high)]
        return jnp.concatenate(parts, axis=1)

    def owner(g):
        return jnp.where(g == count - 1, 1, 0) if owns == 2 else 0

    def first_two(base, which, work):
        sources = []
        for step in work:
            density = [
                own_ref[which if k == PACK - 1 else 0, step] * bands[base + k, step]
                for k in range(PACK)
            ]
            sources += [(6 * step + s, v) for s, v in enumerate(swap_thirds(density, side))]
        along_z = [dot(v, thirds_ref[...]).astype(BF16) for _, v in sources]
        along_y = [dot(cas2_ref[...], v) for v in along_z]
        for (plane, _), v in zip(sources, along_y):
            put(plane, v[:side])
            put(plane + PACK, v[side:])

    def screen(r):
        both = [kernel_ref[min(b, side - b)] for b in (2 * r, 2 * r + 1)]
        return jnp.concatenate(both, axis=0)

    def middle_two(rows):
        planes = [
            jnp.concatenate([get_across(2 * r), get_across(2 * r + 1)], axis=0).astype(BF16)
            for r in rows
        ]
        waves = [dot(ahead_ref[...], v) for v in planes]
        waves = [(v * screen(r)).astype(BF16) for r, v in zip(rows, waves)]
        planes = [dot(back_ref[...], v) for v in waves]
        for r, v in zip(rows, planes):
            put_across(2 * r, v[:side])
            put_across(2 * r + 1, v[side:])

    def last_two(base, which, work):
        halves = [
            [
                jnp.concatenate([get(6 * t + s), get(6 * t + PACK + s)], axis=0).astype(BF16)
                for s in range(PACK)
            ]
            for t in work
        ]
        along_y = [[dot(cas2_ref[...], v).astype(BF16) for v in vs] for vs in halves]
        swapped = [swap_thirds(vs, side) for vs in along_y]
        potential = [[dot(v, thirds_ref[...]) for v in vs] for vs in swapped]
        for t, vs in zip(work, potential):
            terms = [v * bands[base + k, t].astype(F32) for k, v in enumerate(vs)]
            if owns == 1:
                total_ref[0, t] += terms[0] + terms[1] + terms[2]
            else:
                total_ref[0, t] += terms[0] + terms[1]
                total_ref[which, t] += terms[2]

    for copy in own_copies + band_copies[:PACK]:
        copy.wait()
    kernel_copy.start()
    start_copies = [
        pltpu.make_async_copy(ref, total_ref.at[i], wide_sem.at[1 + i]) for i, ref in enumerate(starts)
    ]
    for copy in start_copies:
        copy.start()
    for copy in band_copies[PACK:]:
        copy.start()

    def group(g, carry):
        base = g * PACK
        for k in range(PACK):

            @pl.when((g > 0) & (base + k < len(places)))
            def _(k=k):
                pltpu.make_async_copy(
                    arrays[0].at[0], bands.at[base + k], band_sem.at[base + k]
                ).wait()
        first_two(base, owner(g), list(range(steps)))

        @pl.when(g == 0)
        def _():
            kernel_copy.wait()
            for copy in start_copies:
                copy.wait()

        middle_two(list(range(half)))
        last_two(base, owner(g), list(range(steps)))
        return carry

    lax.fori_loop(0, count, group, 0)
    if totals:
        for k, out_ref in enumerate(out_refs[:cuts]):
            size = out_ref.shape[1]
            out_ref[0] = total_ref[0, k * size : (k + 1) * size].astype(out_ref.dtype)
        for out_ref in out_refs[cuts:]:
            out_ref[...] = total_ref[1]


def solve(own, bands, start, tables, side, cuts=0, second=None):
    owns = 1 if second is None else 2
    levels = len(own)
    starts = [] if start is None else [start]
    if second is not None:
        own, starts = own + second[0], starts + [second[1]]
    places = [(a, k) for a, array in enumerate(bands) for k in range(array.shape[0])]
    shape = (own[0].shape[1] * levels,) + own[0].shape[2:]
    pitch = side + 4
    count = -(-len(places) // PACK)
    vmem = pl.BlockSpec(memory_space=pltpu.VMEM)
    hbm = pl.BlockSpec(memory_space=pl.ANY)
    first = [*own, *bands, *starts, tables[0]]
    body = functools.partial(
        solve_body, side=side, pitch=pitch, places=places, pieces=levels, owns=owns,
        count=count, has_start=start is not None, cuts=cuts
    )
    scratch = [
        pltpu.VMEM((owns,) + shape, BF16),
        pltpu.VMEM((count * PACK,) + shape, BF16),
        pltpu.VMEM(tables[0].shape, F32),
        pltpu.VMEM((side * pitch, HALF), F32),
        pltpu.VMEM((side * pitch, HALF), F32),
        pltpu.SemaphoreType.DMA((len(own),)),
        pltpu.SemaphoreType.DMA((count * PACK,)),
        pltpu.SemaphoreType.DMA((3,)),
    ]
    total = jax.ShapeDtypeStruct(shape, F32)
    piece = jax.ShapeDtypeStruct((1, shape[0] // max(cuts, 1)) + shape[1:], BF16)
    outs = [piece] * cuts + [total] * (owns - 1) if cuts else [jax.ShapeDtypeStruct((1,) + shape, F32)]
    result = pl.pallas_call(
        body,
        in_specs=[hbm] * len(first) + [vmem] * 4,
        out_specs=[vmem] * len(outs),
        out_shape=outs,
        scratch_shapes=scratch + ([pltpu.VMEM((owns,) + shape, F32)] if cuts else []),
        compiler_params=pltpu.CompilerParams(vmem_limit_bytes=60 * 2**20),
        cost_estimate=pl.CostEstimate(
            flops=len(places) * 96 * side**4, bytes_accessed=10 * 2**20, transcendentals=0
        ),
    )(*first, *tables[1:])
    return result if cuts else result[0].reshape(shape)


def make_tables(side, slab, level):
    cas = cas_table(side)
    two = np.eye(2, dtype=np.float32)
    cas2 = jnp.asarray(np.kron(two, cas.astype(np.float32)).astype(BF16))
    three = np.kron(np.eye(PACK, dtype=np.float32), cas.astype(np.float32))
    margin = LANES - three.shape[0]
    thirds = jnp.asarray(np.pad(three, ((0, margin), (0, margin))).astype(BF16))
    screen = screened_kernel(side)[: side // 2 + 1]
    screen = padded(np.concatenate([screen] * PACK, axis=-1), LANES)
    screen = jnp.asarray(screen)
    table = jnp.asarray(cas)
    moved = lax.dynamic_slice_in_dim(jnp.concatenate([table, table], 0), level * slab, side, 0)
    zero = jnp.zeros_like(moved)
    back = jnp.concatenate(
        [jnp.concatenate([moved, zero], 1), jnp.concatenate([zero, moved], 1)], 0
    )
    return screen, cas2, back.T, back, thirds


def from_level(value, ahead):
    count = lax.axis_size("grid")
    pairs = [((h + ahead) % count, h) for h in range(count)]
    return lax.ppermute(value, "grid", pairs)


def flip(value, bit):
    return lax.ppermute(value, "band", [(b, b ^ bit) for b in range(lax.axis_size("band"))])


def pick(options, index):
    result = options[0]
    for k in range(1, len(options)):
        result = jnp.where(index == k, options[k], result)
    return result


def own_slabs(packed, per_device, which):
    levels = lax.axis_size("grid")
    level = lax.axis_index("grid")
    pieces = []
    for ahead in range(levels):
        start = (level + levels - ahead) % levels * per_device + which
        piece = lax.dynamic_slice_in_dim(packed, start, 1, 0)
        pieces.append(from_level(piece, ahead) if ahead else piece)
    return pieces


def spread(slab):
    levels = lax.axis_size("grid")
    return [slab] + [from_level(slab, ahead) for ahead in range(1, levels)]


def whole(slab):
    return jnp.concatenate(spread(slab), axis=1)


def after(value, *others):
    return lax.optimization_barrier((value, others))[0]


def hand_out(packed, which):
    line = lax.axis_index("band") // 2
    share = packed.shape[0] // 4
    parts = []
    for k in range(4):
        part = lax.dynamic_slice_in_dim(packed, (line ^ k) * share + which, 1, 0)
        parts.append(flip(part, 2 * k) if k else part)
    return parts


def keep(parts, owners):
    band = lax.axis_index("band")
    core, line = band % 2, band // 2
    here, there = owners[core], owners[1 - core]
    mine = pick(parts, line ^ (here // 2))
    other = flip(pick(parts, line ^ (there // 2)), 1)
    return jnp.where(here % 2 == core, mine, other)


def fields_small(packed, owners, tables, side):
    levels = lax.axis_size("grid")
    own0 = own_slabs(packed, 2, 0)
    parts0, own0 = lax.optimization_barrier((hand_out(packed, 0), own0))
    slab0 = keep(parts0, owners)
    slab1 = keep(hand_out(after(packed, parts0), 1), owners)
    slab0, tables = lax.optimization_barrier((slab0, tables))
    mine0 = whole(slab0)
    x0, y0 = flip(mine0, 2), flip(mine0, 4)
    other0 = flip(mine0, 1)
    slabs1 = spread(after(slab1, mine0))
    total0 = solve(own0, [mine0, other0], None, tables, side)
    slabs1[0], total0 = lax.optimization_barrier((slabs1[0], total0))
    mine1 = jnp.concatenate(slabs1, axis=1)
    own1 = own_slabs(after(packed, mine1), 2, 1)
    late = after(mine1, x0, y0)
    x1, y1 = flip(late, 2), flip(late, 4)
    near = [mine1, x0, y0]
    near = near + [flip(v, 1) for v in near]
    total0 = solve(own0, near, total0, tables, side)
    x1, y1, total0 = lax.optimization_barrier((x1, y1, total0))
    corner = [flip(after(x0, x1, y1), 4), flip(y1, 2)]
    far = [x1, y1, flip(x1, 1), flip(y1, 1)]
    total1 = solve(own1, [mine0, other0] + near + [x1], None, tables, side)
    corner, total1 = lax.optimization_barrier((corner, total1))
    far = far + corner + [flip(v, 1) for v in corner]
    *field0, total1 = solve(own0, far + far[1:2], total0, tables, side, levels, (own1, total1))
    field1 = solve(own1, far[2:], total1, tables, side, levels)
    return [field0, field1]


def fields_any(packed, owners, tables, side):
    band = lax.axis_index("band")
    levels = lax.axis_size("grid")
    per_device = packed.shape[0] // levels
    own = [own_slabs(packed, per_device, i) for i in range(per_device)]
    totals = [None] * per_device
    for r in range(owners.shape[0]):
        kept = jnp.where(band == owners[r], packed, jnp.zeros_like(packed))
        bands = whole(lax.psum(kept, "band"))
        cuts = levels if r == owners.shape[0] - 1 else 0
        totals = [solve(o, [bands], t, tables, side, cuts) for o, t in zip(own, totals)]
    return totals


def body(orbitals, owners):
    band_count, slab, plane = orbitals.shape
    levels = lax.axis_size("grid")
    level = lax.axis_index("grid")
    side = slab * levels
    tables = make_tables(side, slab, level)
    packed = pack(orbitals, side)
    small = (lax.axis_size("band"), owners.shape[0], band_count, levels) == (8, 2, 8, 4)
    fields = (fields_small if small else fields_any)(packed, owners, tables, side)
    pieces = []
    for field in fields:
        for ahead in range(levels):
            piece = field[(levels - ahead) % levels]
            pieces.append(from_level(piece, ahead) if ahead else piece)
    return unpack(pieces, level, side, len(fields))


def solution(mesh):
    placed = (P("band", "grid", None), P())
    return jax.shard_map(
        body, mesh=mesh, in_specs=placed, out_specs=P("band", "grid", None), check_vma=False
    )
```

```python
import functools
import math

import jax
import jax.numpy as jnp
import numpy as np
from jax import lax
from jax.experimental import pallas as pl
from jax.experimental.pallas import tpu as pltpu
from jax.sharding import PartitionSpec as P

box_length = 12.0
screening = 0.106
BF16 = jnp.bfloat16
F32 = jnp.float32
LANES = 256
HALF = 128
PACK = 3


def cas_table(length):
    points = np.arange(length)
    products = points[:, None] * points[None, :] % length
    phase = products.astype(np.float32) * np.float32(2.0 * math.pi / length)
    return (np.cos(phase) + np.sin(phase)).astype(BF16)


def screened_kernel(length):
    points = np.arange(length)
    folded = np.minimum(points, length - points).astype(np.float32)
    squares = folded * folded
    factor = np.float32((2.0 * math.pi / box_length) ** 2)
    wave_sq = factor * (squares[:, None, None] + squares[None, :, None] + squares[None, None, :])
    positive = np.where(wave_sq > 0.0, wave_sq, np.float32(1.0))
    screen = np.float32(4.0 * math.pi) * (
        np.float32(1.0) - np.exp(-positive / np.float32(4.0 * screening * screening))
    )
    screen = screen / positive / np.float32(length**3)
    return np.where(wave_sq > 0.0, screen, np.float32(0.0)).astype(np.float32)


def padded(array, width):
    return np.pad(array, [(0, 0)] * (array.ndim - 1) + [(0, width - array.shape[-1])])


def pack_body(in_ref, out_ref, rows, *, side):
    planes, bands = in_ref.shape[:2]
    pitch = rows.shape[0] // (planes * bands)
    for x in range(planes):
        values = in_ref[x].astype(F32)
        for y in range(side):
            part = values[:, y * side : (y + 1) * side]
            rows[pl.ds(x * bands * pitch + y, bands, stride=pitch), pl.ds(0, side)] = part
    pad = jnp.zeros((2 * side, LANES - PACK * side), BF16)
    for band in range(bands):
        parts = []
        for s in range(PACK):
            starts = [((PACK * e + s) * bands + band) * pitch for e in range(2)]
            both = [rows[pl.ds(start, side), :][:, :side] for start in starts]
            parts.append(jnp.concatenate(both, axis=0).astype(BF16))
        out_ref[band, 0] = jnp.concatenate(parts + [pad], axis=1)


def pack(orbitals, side):
    count, slab, plane = orbitals.shape
    steps = slab // (2 * PACK)
    return pl.pallas_call(
        functools.partial(pack_body, side=side),
        grid=(steps,),
        in_specs=[pl.BlockSpec((2 * PACK, count, plane), lambda m: (m, 0, 0))],
        out_specs=pl.BlockSpec((count, 1, 2 * side, LANES), lambda m: (0, m, 0, 0)),
        out_shape=jax.ShapeDtypeStruct((count, steps, 2 * side, LANES), BF16),
        scratch_shapes=[pltpu.VMEM((2 * PACK * count * (side + 4), HALF), F32)],
        compiler_params=pltpu.CompilerParams(vmem_limit_bytes=32 * 2**20),
    )(orbitals.transpose(1, 0, 2))


def unpack_body(level_ref, *refs, side, levels):
    pieces, (out_ref, rows) = refs[:-2], refs[-2:]
    planes, bands = out_ref.shape[:2]
    share = bands // levels
    pitch = rows.shape[0] // (planes * bands)
    for k, piece in enumerate(pieces):
        band = (level_ref[0] + k % levels) % levels * share + k // levels
        value = piece[0, 0].astype(F32)
        for s in range(PACK):
            part = value[:, s * side : (s + 1) * side]
            for e in range(2):
                start = ((PACK * e + s) * bands + band) * pitch
                rows[pl.ds(start, side), pl.ds(0, side)] = part[e * side : (e + 1) * side]
    for x in range(planes):
        parts = [rows[pl.ds(x * bands * pitch + y, bands, stride=pitch), :] for y in range(side)]
        out_ref[x] = jnp.concatenate([v[:, :side] for v in parts], axis=1)


def unpack(pieces, level, side, share):
    levels = len(pieces) // share
    bands = len(pieces)
    steps = pieces[0].shape[1]
    grid_spec = pltpu.PrefetchScalarGridSpec(
        num_scalar_prefetch=1,
        grid=(steps,),
        in_specs=[pl.BlockSpec((1, 1, 2 * side, LANES), lambda m, first: (0, m, 0, 0))] * bands,
        out_specs=pl.BlockSpec((2 * PACK, bands, side * side), lambda m, first: (m, 0, 0)),
        scratch_shapes=[pltpu.VMEM((2 * PACK * bands * (side + 4), HALF), F32)],
    )
    field = pl.pallas_call(
        functools.partial(unpack_body, side=side, levels=levels),
        grid_spec=grid_spec,
        out_shape=jax.ShapeDtypeStruct((2 * PACK * steps, bands, side * side), F32),
        compiler_params=pltpu.CompilerParams(vmem_limit_bytes=32 * 2**20),
    )(jnp.reshape(level, (1,)), *pieces)
    return field.transpose(1, 0, 2)


def dot(left, right):
    return lax.dot_general(left, right, (((1,), (0,)), ((), ())), preferred_element_type=F32)


def swap_thirds(values, side):
    pad = jnp.zeros((values[0].shape[0], LANES - PACK * side), values[0].dtype)
    return [
        jnp.concatenate([v[:, side * s : side * s + side] for v in values] + [pad], axis=1)
        for s in range(PACK)
    ]


def solve_body(*refs, side, pitch, places, pieces, owns, count, has_start, cuts):
    own_pieces, rest = refs[: pieces * owns], refs[pieces * owns :]
    arrays = rest[: max(a for a, _ in places) + 1]
    rest = rest[len(arrays) :]
    starts, rest = rest[: owns * has_start], rest[owns * has_start :]
    kernel_hbm, cas2_ref, ahead_ref, back_ref, thirds_ref = rest[:5]
    out_refs = rest[5 : 4 + max(cuts, 1) + owns]
    own_ref, bands, kernel_ref, low, high, own_sem, band_sem, wide_sem, *totals = rest[5 + len(out_refs) :]
    total_ref = totals[0] if totals else out_refs[0]
    steps = own_ref.shape[1]
    half = side // 2
    part = steps // pieces

    own_copies = [
        pltpu.make_async_copy(
            ref.at[0], own_ref.at[k // pieces, pl.ds(k % pieces * part, part)], own_sem.at[k]
        )
        for k, ref in enumerate(own_pieces)
    ]
    band_copies = [
        pltpu.make_async_copy(arrays[a].at[k], bands.at[j], band_sem.at[j])
        for j, (a, k) in enumerate(places)
    ]
    kernel_copy = pltpu.make_async_copy(kernel_hbm, kernel_ref, wide_sem.at[0])
    for copy in own_copies + band_copies[:PACK]:
        copy.start()
    if not has_start:
        total_ref[...] = jnp.zeros_like(total_ref)
    for j in range(len(places), bands.shape[0]):
        bands[j] = jnp.zeros_like(bands[j])

    def put(plane, value):
        low[pl.ds(plane * pitch, side), :] = value[:, :HALF]
        high[pl.ds(plane * pitch, side), :] = value[:, HALF:]

    def get(plane):
        parts = [r[pl.ds(plane * pitch, side), :] for r in (low, high)]
        return jnp.concatenate(parts, axis=1)

    def put_across(row, value):
        low[pl.ds(row, side, stride=pitch), :] = value[:, :HALF]
        high[pl.ds(row, side, stride=pitch), :] = value[:, HALF:]

    def get_across(row):
        parts = [r[pl.ds(row, side, stride=pitch), :] for r in (low, high)]
        return jnp.concatenate(parts, axis=1)

    def first_two(base, which, work):
        sources = []
        for step in work:
            density = [
                own_ref[which if k == PACK - 1 else 0, step] * bands[base + k, step]
                for k in range(PACK)
            ]
            sources += [(6 * step + s, v) for s, v in enumerate(swap_thirds(density, side))]
        along_z = [dot(v, thirds_ref[...]).astype(BF16) for _, v in sources]
        along_y = [dot(cas2_ref[...], v) for v in along_z]
        for (plane, _), v in zip(sources, along_y):
            put(plane, v[:side])
            put(plane + PACK, v[side:])

    def screen(r):
        both = [kernel_ref[min(b, side - b)] for b in (2 * r, 2 * r + 1)]
        return jnp.concatenate(both, axis=0)

    def middle_two(rows):
        planes = [
            jnp.concatenate([get_across(2 * r), get_across(2 * r + 1)], axis=0).astype(BF16)
            for r in rows
        ]
        waves = [dot(ahead_ref[...], v) for v in planes]
        waves = [(v * screen(r)).astype(BF16) for r, v in zip(rows, waves)]
        planes = [dot(back_ref[...], v) for v in waves]
        for r, v in zip(rows, planes):
            put_across(2 * r, v[:side])
            put_across(2 * r + 1, v[side:])

    def last_two(base, which, work):
        halves = [
            [
                jnp.concatenate([get(6 * t + s), get(6 * t + PACK + s)], axis=0).astype(BF16)
                for s in range(PACK)
            ]
            for t in work
        ]
        along_y = [[dot(cas2_ref[...], v).astype(BF16) for v in vs] for vs in halves]
        swapped = [swap_thirds(vs, side) for vs in along_y]
        potential = [[dot(v, thirds_ref[...]) for v in vs] for vs in swapped]
        for t, vs in zip(work, potential):
            terms = [v * bands[base + k, t].astype(F32) for k, v in enumerate(vs)]
            if which == 0:
                total_ref[0, t] += terms[0] + terms[1] + terms[2]
            else:
                total_ref[0, t] += terms[0] + terms[1]
                total_ref[which, t] += terms[2]

    for copy in own_copies + band_copies[:PACK]:
        copy.wait()
    kernel_copy.start()
    start_copies = [
        pltpu.make_async_copy(ref, total_ref.at[i], wide_sem.at[1 + i]) for i, ref in enumerate(starts)
    ]
    for copy in start_copies:
        copy.start()
    for copy in band_copies[PACK:]:
        copy.start()

    def group(g, carry, which=0):
        base = g * PACK
        for k in range(PACK):

            @pl.when((g > 0) & (base + k < len(places)))
            def _(k=k):
                pltpu.make_async_copy(
                    arrays[0].at[0], bands.at[base + k], band_sem.at[base + k]
                ).wait()
        first_two(base, which, list(range(steps)))

        @pl.when(g == 0)
        def _():
            kernel_copy.wait()
            for copy in start_copies:
                copy.wait()

        middle_two(list(range(half)))
        last_two(base, which, list(range(steps)))
        return carry

    lax.fori_loop(0, count - (owns - 1), group, 0)
    if owns == 2:
        group(jnp.int32(count - 1), 0, 1)
    if totals:
        for k, out_ref in enumerate(out_refs[:cuts]):
            size = out_ref.shape[1]
            out_ref[0] = total_ref[0, k * size : (k + 1) * size].astype(out_ref.dtype)
        for out_ref in out_refs[cuts:]:
            out_ref[...] = total_ref[1]


def solve(own, bands, start, tables, side, cuts=0, second=None):
    owns = 1 if second is None else 2
    levels = len(own)
    starts = [] if start is None else [start]
    if second is not None:
        own, starts = own + second[0], starts + [second[1]]
    places = [(a, k) for a, array in enumerate(bands) for k in range(array.shape[0])]
    shape = (own[0].shape[1] * levels,) + own[0].shape[2:]
    pitch = side + 4
    count = -(-len(places) // PACK)
    vmem = pl.BlockSpec(memory_space=pltpu.VMEM)
    hbm = pl.BlockSpec(memory_space=pl.ANY)
    first = [*own, *bands, *starts, tables[0]]
    body = functools.partial(
        solve_body, side=side, pitch=pitch, places=places, pieces=levels, owns=owns,
        count=count, has_start=start is not None, cuts=cuts
    )
    scratch = [
        pltpu.VMEM((owns,) + shape, BF16),
        pltpu.VMEM((count * PACK,) + shape, BF16),
        pltpu.VMEM(tables[0].shape, F32),
        pltpu.VMEM((side * pitch, HALF), F32),
        pltpu.VMEM((side * pitch, HALF), F32),
        pltpu.SemaphoreType.DMA((len(own),)),
        pltpu.SemaphoreType.DMA((count * PACK,)),
        pltpu.SemaphoreType.DMA((3,)),
    ]
    total = jax.ShapeDtypeStruct(shape, F32)
    piece = jax.ShapeDtypeStruct((1, shape[0] // max(cuts, 1)) + shape[1:], BF16)
    outs = [piece] * cuts + [total] * (owns - 1) if cuts else [jax.ShapeDtypeStruct((1,) + shape, F32)]
    result = pl.pallas_call(
        body,
        in_specs=[hbm] * len(first) + [vmem] * 4,
        out_specs=[vmem] * len(outs),
        out_shape=outs,
        scratch_shapes=scratch + ([pltpu.VMEM((owns,) + shape, F32)] if cuts else []),
        compiler_params=pltpu.CompilerParams(vmem_limit_bytes=60 * 2**20),
        cost_estimate=pl.CostEstimate(
            flops=len(places) * 96 * side**4, bytes_accessed=10 * 2**20, transcendentals=0
        ),
    )(*first, *tables[1:])
    return result if cuts else result[0].reshape(shape)


def make_tables(side, slab, level):
    cas = cas_table(side)
    two = np.eye(2, dtype=np.float32)
    cas2 = jnp.asarray(np.kron(two, cas.astype(np.float32)).astype(BF16))
    three = np.kron(np.eye(PACK, dtype=np.float32), cas.astype(np.float32))
    margin = LANES - three.shape[0]
    thirds = jnp.asarray(np.pad(three, ((0, margin), (0, margin))).astype(BF16))
    screen = screened_kernel(side)[: side // 2 + 1]
    screen = padded(np.concatenate([screen] * PACK, axis=-1), LANES)
    screen = jnp.asarray(screen)
    table = jnp.asarray(cas)
    moved = lax.dynamic_slice_in_dim(jnp.concatenate([table, table], 0), level * slab, side, 0)
    zero = jnp.zeros_like(moved)
    back = jnp.concatenate(
        [jnp.concatenate([moved, zero], 1), jnp.concatenate([zero, moved], 1)], 0
    )
    return screen, cas2, back.T, back, thirds


def from_level(value, ahead):
    count = lax.axis_size("grid")
    pairs = [((h + ahead) % count, h) for h in range(count)]
    return lax.ppermute(value, "grid", pairs)


def flip(value, bit):
    return lax.ppermute(value, "band", [(b, b ^ bit) for b in range(lax.axis_size("band"))])


def pick(options, index):
    result = options[0]
    for k in range(1, len(options)):
        result = jnp.where(index == k, options[k], result)
    return result


def own_slabs(packed, per_device, which):
    levels = lax.axis_size("grid")
    level = lax.axis_index("grid")
    pieces = []
    for ahead in range(levels):
        start = (level + levels - ahead) % levels * per_device + which
        piece = lax.dynamic_slice_in_dim(packed, start, 1, 0)
        pieces.append(from_level(piece, ahead) if ahead else piece)
    return pieces


def spread(slab):
    levels = lax.axis_size("grid")
    return [slab] + [from_level(slab, ahead) for ahead in range(1, levels)]


def whole(slab):
    return jnp.concatenate(spread(slab), axis=1)


def after(value, *others):
    return lax.optimization_barrier((value, others))[0]


def hand_out(packed, which):
    line = lax.axis_index("band") // 2
    share = packed.shape[0] // 4
    parts = []
    for k in range(4):
        part = lax.dynamic_slice_in_dim(packed, (line ^ k) * share + which, 1, 0)
        parts.append(flip(part, 2 * k) if k else part)
    return parts


def keep(parts, owners):
    band = lax.axis_index("band")
    core, line = band % 2, band // 2
    here, there = owners[core], owners[1 - core]
    mine = pick(parts, line ^ (here // 2))
    other = flip(pick(parts, line ^ (there // 2)), 1)
    return jnp.where(here % 2 == core, mine, other)


def fields_small(packed, owners, tables, side):
    levels = lax.axis_size("grid")
    own0 = own_slabs(packed, 2, 0)
    parts0, own0 = lax.optimization_barrier((hand_out(packed, 0), own0))
    slab0 = keep(parts0, owners)
    slab1 = keep(hand_out(after(packed, parts0), 1), owners)
    slab0, tables = lax.optimization_barrier((slab0, tables))
    mine0 = whole(slab0)
    x0, y0 = flip(mine0, 2), flip(mine0, 4)
    other0 = flip(mine0, 1)
    slabs1 = spread(after(slab1, mine0))
    total0 = solve(own0, [mine0, other0], None, tables, side)
    slabs1[0], total0 = lax.optimization_barrier((slabs1[0], total0))
    mine1 = jnp.concatenate(slabs1, axis=1)
    own1 = own_slabs(after(packed, mine1), 2, 1)
    late = after(mine1, x0, y0)
    x1, y1 = flip(late, 2), flip(late, 4)
    near = [mine1, x0, y0]
    near = near + [flip(v, 1) for v in near]
    total0 = solve(own0, near, total0, tables, side)
    x1, y1, total0 = lax.optimization_barrier((x1, y1, total0))
    corner = [flip(after(x0, x1, y1), 4), flip(y1, 2)]
    far = [x1, y1, flip(x1, 1), flip(y1, 1)]
    total1 = solve(own1, [mine0, other0] + near + [x1], None, tables, side)
    corner, total1 = lax.optimization_barrier((corner, total1))
    far = far + corner + [flip(v, 1) for v in corner]
    *field0, total1 = solve(own0, far + far[1:2], total0, tables, side, levels, (own1, total1))
    field1 = solve(own1, far[2:], total1, tables, side, levels)
    return [field0, field1]


def fields_any(packed, owners, tables, side):
    band = lax.axis_index("band")
    levels = lax.axis_size("grid")
    per_device = packed.shape[0] // levels
    own = [own_slabs(packed, per_device, i) for i in range(per_device)]
    totals = [None] * per_device
    for r in range(owners.shape[0]):
        kept = jnp.where(band == owners[r], packed, jnp.zeros_like(packed))
        bands = whole(lax.psum(kept, "band"))
        cuts = levels if r == owners.shape[0] - 1 else 0
        totals = [solve(o, [bands], t, tables, side, cuts) for o, t in zip(own, totals)]
    return totals


def body(orbitals, owners):
    band_count, slab, plane = orbitals.shape
    levels = lax.axis_size("grid")
    level = lax.axis_index("grid")
    side = slab * levels
    tables = make_tables(side, slab, level)
    packed = pack(orbitals, side)
    small = (lax.axis_size("band"), owners.shape[0], band_count, levels) == (8, 2, 8, 4)
    fields = (fields_small if small else fields_any)(packed, owners, tables, side)
    pieces = []
    for field in fields:
        for ahead in range(levels):
            piece = field[(levels - ahead) % levels]
            pieces.append(from_level(piece, ahead) if ahead else piece)
    return unpack(pieces, level, side, len(fields))


def solution(mesh):
    placed = (P("band", "grid", None), P())
    return jax.shard_map(
        body, mesh=mesh, in_specs=placed, out_specs=P("band", "grid", None), check_vma=False
    )
```
